32 devices in a mesh: depth: 4 (over z), tile: 8 (over y, x, core).
Axes of the slice: x: 2, y: 2, z: 4, core: 2. Of those that a mesh axis runs over, the one named last changes fastest.
Arguments:
- volume: bfloat16 [512, 64, 1024], P(None, 'depth', 'tile'), may hold values from -6 to 6
- active: int32 [4, 8], P('depth', 'tile'), may hold values 0 or 1
- depth_order: int32 [2, 4], replicated, may hold values from 0 to 3, each once within a row
- light_vector: float32 [2, 3], replicated, may hold values from -4 to 4
- class_gain: float32 [4], replicated, may hold values from 0.5 to 2
- class_bias: float32 [4], replicated, may hold values from -1 to 1
Outputs:
- image: float32 [2, 4, 512, 1024], P(None, None, ('depth', 'tile'))
The draws below stay inside these ranges and needn't reach their ends.
Inputs may be any that keep to these rules, and one draw needn't show every extreme that they name: Each row of depth_order lists every slab group exactly once; depth_order[v, r] is the group at the r-th place from the eye in view v. `active`: A 0 marks a brick whose voxels are empty.
All inputs are finite; a program needn't handle non-finite values. No bound on the sum of `active` on one device may be relied on, other than what follows from the above.
Results may differ from the reference program's by a relative error of at most 0.0013.
Values may be sent and summed in bfloat16 or wider, within the bound.
No kernel may reach another device: no remote copies, remote signals or barrier semaphores. Data moves between devices by JAX's collectives and lax.ppermute only.
A program may use at most 64 MiB of HBM per device.

```python
import jax
import jax.numpy as jnp
from jax import lax

BY = 512
BZ = 16
BX = 128
VIEWS = 2
NZ = 64
NX = 1024
N_DEPTH = 4
N_TILE = 8


def with_ends(values, stream_key, smallest, high):
    place = [jax.random.randint(jax.random.fold_in(stream_key, axis), (), 0, length) for axis, length in enumerate(values.shape)]
    longest = values.shape.index(max(values.shape))
    neighbour = place[:longest] + [(place[longest] + 1) % values.shape[longest]] + place[longest + 1:]
    return values.at[tuple(place)].set(smallest).at[tuple(neighbour)].set(high)


def levels(own_key, extent, cuts, smallest, largest):
    def one(dim, parts):
        steps = jax.random.uniform(jax.random.fold_in(jax.random.fold_in(own_key, 6), dim), (parts,), jnp.float32, smallest / len(cuts), largest / len(cuts))
        return jnp.repeat(jnp.exp(steps), extent[dim] // parts).reshape((-1,) + (1,) * (len(extent) - dim - 1))

    factor_of = one(*cuts[0])
    for cut in cuts[1:]:
        factor_of = factor_of * one(*cut)
    return factor_of


def bell_draw(key, extent, spread, limit, cuts=(), kind=jnp.bfloat16):
    values = jax.random.normal(key, extent, jnp.float32) * spread
    if len(cuts) > 0:
        values = levels(key, extent, cuts, -0.22, 0.18) * values
    return jnp.clip(values, min=-limit, max=limit).astype(kind)


def setup_inputs(seed: int = 0) -> dict:
    key_of = jax.random.split(jax.random.key(seed), 7)
    volume = bell_draw(key_of[0], (BY, NZ, NX), 1.0, 6.0, ((1, 4), (2, 8)))
    active = with_ends((jax.random.randint(key_of[1], (N_DEPTH, N_TILE), 0, 4) < 3).astype(jnp.int32), jax.random.fold_in(key_of[1], 1), 0, 1)
    depth_order = jax.vmap(lambda own: jax.random.permutation(own, N_DEPTH))(jax.random.split(key_of[2], VIEWS)).reshape((VIEWS, N_DEPTH)).astype(jnp.int32)
    light_vector = bell_draw(key_of[3], (VIEWS, 3), 1.0, 4.0, (), jnp.float32)
    class_gain = jnp.clip(jax.random.uniform(key_of[4], (4,), jnp.float32, 0.5, 2.0), 0.5, 2.0)
    class_bias = jnp.clip(jax.random.uniform(key_of[5], (4,), jnp.float32, -1.0, 1.0), -1.0, 1.0)
    return dict(volume=volume, active=active, depth_order=depth_order, light_vector=light_vector, class_gain=class_gain, class_bias=class_bias)


row_block = 16

def shear_rows(stacked, offset_step):
    leading = stacked.shape[:-2]
    slices, columns = stacked.shape[-2:]
    period = 2 * columns + offset_step
    widths = [(0, 0)] * (len(leading) + 1) + [(0, period - columns)]
    padded = jnp.pad(stacked, widths)
    flattened = padded.reshape(leading + (slices * period,))
    trimmed = flattened[..., :slices * 2 * columns]
    return trimmed.reshape(leading + (slices, 2 * columns))

def shade_block(block, weight_on, light_vector, class_gain, class_bias, total_z, views):
    field = block.astype(jnp.float32)
    center = field[1:-1, :, 1:-1]
    grad_x = 0.5 * (field[1:-1, :, 2:] - field[1:-1, :, :-2])
    grad_y = 0.5 * (field[2:, :, 1:-1] - field[:-2, :, 1:-1])
    zpadded = jnp.pad(center, ((0, 0), (1, 1), (0, 0)))
    grad_z = 0.5 * (zpadded[:, 2:] - zpadded[:, :-2])
    grad_sq = grad_x * grad_x + grad_y * grad_y + grad_z * grad_z
    sigma = weight_on * 2.0 * jax.nn.softplus(class_gain[3] * center + class_bias[3]) / total_z
    tints = [jax.nn.sigmoid(class_gain[channel] * center + class_bias[channel]) for channel in range(3)]
    slices = center.shape[1]
    columns = center.shape[2]
    results = []
    for view_index in range(views):
        light_x = light_vector[view_index, 0]
        light_y = light_vector[view_index, 1]
        light_z = light_vector[view_index, 2]
        length_sq = light_x * light_x + light_y * light_y + light_z * light_z
        facing = grad_x * light_x + grad_y * light_y + grad_z * light_z
        shade = 0.3 + 0.7 * jnp.abs(facing) / jnp.sqrt(grad_sq * length_sq + 1.0)
        stacked = jnp.stack([sigma * tints[0] * shade, sigma * tints[1] * shade, sigma * tints[2] * shade, sigma])
        sheared = shear_rows(stacked, (view_index + 1) * columns // (2 * slices))
        optical = sheared[3]
        before = jnp.cumsum(optical, axis=1) - optical
        through = jnp.exp(-before)
        colour = lax.optimization_barrier(jnp.sum(sheared[:3] * through[None], axis=2))
        depth_sum = lax.optimization_barrier(jnp.sum(optical, axis=1))
        results.append(jnp.concatenate([colour, depth_sum[None]], axis=0))
    return jnp.stack(results)

def footprint(padded_x, weight_on, light_vector, class_gain, class_bias, total_z):
    rows = padded_x.shape[0]
    blocks = rows // row_block
    views = light_vector.shape[0]
    ypadded = jnp.pad(padded_x, ((1, 1), (0, 0), (0, 0)))

    def one_block(block_index):
        block = lax.dynamic_slice_in_dim(ypadded, block_index * row_block, row_block + 2, 0)
        return shade_block(block, weight_on, light_vector, class_gain, class_bias, total_z, views)
    stacked = lax.map(one_block, jnp.arange(blocks, dtype=jnp.int32))
    return jnp.transpose(stacked, (1, 2, 0, 3, 4)).reshape(views, 4, rows, stacked.shape[-1])

def over(front, back, axis):
    front_color = lax.slice_in_dim(front, 0, 3, axis=axis)
    front_depth = lax.slice_in_dim(front, 3, 4, axis=axis)
    back_color = lax.slice_in_dim(back, 0, 3, axis=axis)
    back_depth = lax.slice_in_dim(back, 3, 4, axis=axis)
    return jnp.concatenate([front_color + jnp.exp(-front_depth) * back_color, front_depth + back_depth], axis=axis)

def composite(layers, depth_order):
    groups = layers.shape[0]
    group_ids = jnp.arange(groups, dtype=jnp.int32)
    places = lax.optimization_barrier(jnp.sum(jnp.where(depth_order[:, :, None] == group_ids[None, None, :], group_ids[None, :, None], 0), axis=1))
    ahead = (places[:, None, :] < places[:, :, None]).astype(jnp.float32)
    depths = layers[:, :, 3]
    front = jnp.einsum('vgh,hvrc->gvrc', ahead, depths, precision=lax.Precision.HIGHEST)
    colour = lax.optimization_barrier(jnp.sum(layers[:, :, :3] * jnp.exp(-front)[:, :, None], axis=0))
    total = lax.optimization_barrier(jnp.sum(depths, axis=0))
    return jnp.concatenate([colour, (1.0 - jnp.exp(-total))[:, None]], axis=1)

def reference(volume, active, depth_order, light_vector, class_gain, class_bias):
    rows, depth_cells, width_cells = volume.shape
    views = light_vector.shape[0]
    xpadded = jnp.pad(volume, ((0, 0), (0, 0), (1, 1)))

    def one_brick(brick_index):
        slab = brick_index // N_TILE
        column = brick_index % N_TILE
        starts = (jnp.int32(0), (slab * BZ).astype(jnp.int32), (column * BX).astype(jnp.int32))
        brick = lax.dynamic_slice(xpadded, starts, (rows, BZ, BX + 2))
        weight_on = active[slab, column].astype(jnp.float32)
        return footprint(brick, weight_on, light_vector, class_gain, class_bias, depth_cells)
    prints = lax.map(one_brick, jnp.arange(N_DEPTH * N_TILE, dtype=jnp.int32))
    prints = prints.reshape(N_DEPTH, N_TILE, views, 4, rows, 2, BX)
    prints = jnp.transpose(prints, (0, 2, 3, 4, 1, 5, 6))
    own = prints[:, :, :, :, :, 0]
    spill = prints[:, :, :, :, :, 1]
    spill = jnp.pad(spill[:, :, :, :, :-1], ((0, 0), (0, 0), (0, 0), (0, 0), (1, 0), (0, 0)))
    layers = over(own, spill, 2).reshape(N_DEPTH, views, 4, rows, N_TILE * BX)
    return composite(layers, depth_order)
```

```python
import functools
import jax
import jax.numpy as jnp
from jax import lax
from jax.experimental import pallas as pl
from jax.experimental.pallas import tpu as pltpu
from jax.sharding import PartitionSpec as P

group = 8


def softplus(u):
    w = jnp.exp(u)
    return jnp.where(w < 0.004, w * (1.0 - 0.5 * w), jnp.log(1.0 + w))


def print_kernel(views, total_z, first_ref, active_ref, light_ref, gain_ref, bias_ref, volume_ref, halo_ref,
                 mix_ref, own_ref, over_ref, field, slope):
    rows = own_ref.shape[2]
    all_rows, slices, columns = volume_ref.shape
    first = first_ref[0]
    mix = mix_ref[...]

    def prepare(block, count, start):
        both = jnp.dot(block.reshape(count * slices, columns), mix, preferred_element_type=jnp.float32)
        at = pl.ds(start, count * slices)
        field[at, :] = both[:, :columns]
        slope[at, :] = both[:, columns:]

    def edge(row, start):
        inside = jnp.logical_and(row >= 0, row < all_rows)
        kept = jnp.clip(row, 0, all_rows - 1)
        block = volume_ref[pl.ds(kept, 1)].astype(jnp.float32)
        field[pl.ds(start, slices), :] = jnp.where(inside, block, 0.0).reshape(slices, columns)

    edge(first - 1, 0)
    edge(first + rows, (rows + 1) * slices)

    def fill(step, carry):
        at = pl.multiple_of(step * group, group)
        block = volume_ref[pl.ds(first + at, group)]
        prepare(block, group, pl.multiple_of((at + 1) * slices, group * slices // 8))
        return carry

    lax.fori_loop(0, rows // group, fill, 0)

    weight = active_ref[0, 0].astype(jnp.float32) * (1.0 / total_z)
    half_gain = [0.5 * gain_ref[k] for k in range(3)]
    half_bias = [0.5 * bias_ref[k] for k in range(3)]
    squares = []
    slants = []
    for v in range(views):
        parts = [light_ref[v, k] for k in range(3)]
        squares.append(0.25 * (parts[0] * parts[0] + parts[1] * parts[1] + parts[2] * parts[2]))
        slants.append([0.35 * part for part in parts])
    lane = lax.broadcasted_iota(jnp.int32, (group, columns), 1)
    rim = jnp.logical_or(lane == 0, lane == columns - 1)
    shears = [(v + 1) * columns // (2 * slices) for v in range(views)]

    def work(step, carry):
        at = pl.multiple_of(step * group, group)
        base = (at + 1) * slices
        halo = halo_ref[pl.ds(pl.multiple_of(first + at, group), group), :]

        def rows_of(ref, z, shift):
            return ref[pl.ds(base + shift * slices + z, group, stride=slices), :]

        zero = jnp.zeros((group, columns), jnp.float32)
        colours = [[zero] * 3 for _ in range(views)]
        before = [zero] * views
        behind = zero
        here = rows_of(field, 0, 0)
        for z in range(slices):
            ahead = rows_of(field, z + 1, 0) if z + 1 < slices else zero
            dy = rows_of(field, z, 1) - rows_of(field, z, -1)
            side = halo if z == 0 else pltpu.roll(halo, columns - 2 * z, 1)
            dx = rows_of(slope, z, 0) + jnp.where(rim, side, 0.0)
            dz = ahead - behind
            steep = dx * dx + dy * dy + dz * dz
            sigma = weight * 2.0 * softplus(gain_ref[3] * here + bias_ref[3])
            half = 0.5 * sigma
            tinted = [half + half * jnp.tanh(half_gain[k] * here + half_bias[k]) for k in range(3)]
            for v in range(views):
                lx, ly, lz = slants[v]
                facing = dx * lx + dy * ly + dz * lz
                shade = 0.3 + jnp.abs(facing) * lax.rsqrt(steep * squares[v] + 1.0)
                by = z * shears[v]
                glow = [part * shade for part in tinted]
                thick = sigma
                if by:
                    glow = [pltpu.roll(part, by, 1) for part in glow]
                    thick = pltpu.roll(sigma, by, 1)
                    crossed = jnp.logical_and(lane >= by - shears[v], lane < by)
                    for k in range(3):
                        pltpu.store(own_ref.at[v, k, pl.ds(at, group), :], colours[v][k], mask=crossed)
                    pltpu.store(own_ref.at[v, 3, pl.ds(at, group), :], before[v], mask=crossed)
                    before[v] = jnp.where(crossed, 0.0, before[v])
                through = jnp.exp(-before[v])
                for k in range(3):
                    colours[v][k] = colours[v][k] + glow[k] * through
                before[v] = before[v] + thick
            behind, here = here, ahead
        for v in range(views):
            whole = lane >= (slices - 1) * shears[v]
            finals = colours[v] + [before[v]]
            for k in range(4):
                row_at = (v, k, pl.ds(at, group), slice(None))
                pltpu.store(own_ref.at[v, k, pl.ds(at, group), :], finals[k], mask=whole)
                rest = finals[k] if k == 3 else finals[k] - own_ref[row_at]
                over_ref[row_at] = jnp.where(whole, 0.0, rest)
        return carry

    lax.fori_loop(0, rows // group, work, 0)


def prints_of(volume, halo, first, rows, active, light_vector, class_gain, class_bias, total_z):
    all_rows, slices, columns = volume.shape
    views = light_vector.shape[0]
    i = jnp.arange(columns)
    eye = (i[:, None] == i[None, :])
    diff = (i[:, None] == i[None, :] + 1).astype(jnp.bfloat16) - (i[:, None] == i[None, :] - 1).astype(jnp.bfloat16)
    mix = jnp.concatenate([eye.astype(jnp.bfloat16), diff], axis=1)
    smem = pl.BlockSpec(memory_space=pltpu.SMEM)
    vmem = pl.BlockSpec(memory_space=pltpu.VMEM)
    shape = jax.ShapeDtypeStruct((views, 4, rows, columns), jnp.float32)
    return pl.pallas_call(
        functools.partial(print_kernel, views, total_z),
        out_shape=[shape, shape],
        in_specs=[smem] * 5 + [vmem] * 3,
        out_specs=[vmem, vmem],
        scratch_shapes=[pltpu.VMEM(((rows + 2) * slices, columns), jnp.float32)] * 2,
        compiler_params=pltpu.CompilerParams(vmem_limit_bytes=40 * 1024 * 1024),
        name="prints",
    )(first, active, light_vector, class_gain, class_bias, volume, halo, mix)


def passed_along(x, axis, by):
    devices = lax.axis_size(axis)
    pairs = [(i, i + by) for i in range(devices) if 0 <= i + by < devices]
    return lax.ppermute(x, axis, pairs)


def halo_rows(volume):
    columns = volume.shape[2]
    left = passed_along(volume[:, :, -1], "tile", 1).astype(jnp.float32)
    right = passed_along(volume[:, :, 0], "tile", -1).astype(jnp.float32)
    woven = jnp.stack([-left, jnp.roll(right, -1, axis=1)], axis=2).reshape(left.shape[0], -1)
    gap = jnp.zeros((left.shape[0], columns - 1 - woven.shape[1]), jnp.float32)
    return jnp.concatenate([woven, gap, right[:, :1]], axis=1)


def over(front, back, axis):
    front_color = lax.slice_in_dim(front, 0, 3, axis=axis)
    front_depth = lax.slice_in_dim(front, 3, 4, axis=axis)
    back_color = lax.slice_in_dim(back, 0, 3, axis=axis)
    back_depth = lax.slice_in_dim(back, 3, 4, axis=axis)
    return jnp.concatenate(
        [front_color + jnp.exp(-front_depth) * back_color, front_depth + back_depth], axis=axis
    )


def composite(layers, depth_order):
    groups = layers.shape[0]
    group_ids = jnp.arange(groups, dtype=jnp.int32)
    places = jnp.sum(
        jnp.where(depth_order[:, :, None] == group_ids[None, None, :], group_ids[None, :, None], 0),
        axis=1,
    )
    ahead = (places[:, None, :] < places[:, :, None]).astype(jnp.float32)
    depths = layers[:, :, 3]
    front = jnp.einsum("vgh,hvrc->gvrc", ahead, depths, precision=lax.Precision.HIGHEST)
    colour = jnp.sum(layers[:, :, :3] * jnp.exp(-front)[:, :, None], axis=0)
    total = jnp.sum(depths, axis=0)
    return jnp.concatenate([colour, (1.0 - jnp.exp(-total))[:, None]], axis=1)


def local(volume, active, depth_order, light_vector, class_gain, class_bias):
    depth_count = lax.axis_size("depth")
    tile_count = lax.axis_size("tile")
    rows, slices, width = volume.shape
    total_z = slices * depth_count
    share = rows // (depth_count * tile_count)
    halo = halo_rows(volume)
    first = jnp.zeros((1,), jnp.int32)
    own, overhang = prints_of(volume, halo, first, rows, active, light_vector, class_gain, class_bias, total_z)
    views, channels = own.shape[:2]
    arrived = passed_along(overhang.astype(jnp.bfloat16), "tile", 1).astype(overhang.dtype)
    merged = over(own, arrived, 1)
    received = lax.all_to_all(merged, ("depth", "tile"), split_axis=2, concat_axis=3, tiled=True)
    every = received.reshape(views, channels, share, depth_count, tile_count * width)
    every = jnp.transpose(every, (3, 0, 1, 2, 4))
    return composite(every, depth_order)


def solution(mesh):
    placed = (P(None, "depth", "tile"), P("depth", "tile"), P(), P(), P(), P())
    return jax.shard_map(
        local,
        mesh=mesh,
        in_specs=placed,
        out_specs=P(None, None, ("depth", "tile"), None),
        check_vma=False,
    )
```

```python
import functools
import math
import jax
import jax.numpy as jnp
from jax import lax
from jax.experimental import pallas as pl
from jax.experimental.pallas import tpu as pltpu
from jax.sharding import PartitionSpec as P

LN2 = math.log(2.0)
code_step = 1638.0
code_middle = 16.0
code_none = -32768.0

smem = pl.BlockSpec(memory_space=pltpu.SMEM)
vmem = pl.BlockSpec(memory_space=pltpu.VMEM)
params = pltpu.CompilerParams(vmem_limit_bytes=24 * 1024 * 1024)


def encode(x):
    return jnp.round(jnp.maximum(code_step * lax.log2(x) + code_step * code_middle, code_none)).astype(jnp.int16)


def decode(q):
    value = q.astype(jnp.int32).astype(jnp.float32)
    return jnp.where(value == code_none, 0.0, lax.exp2(value * (1.0 / code_step) - code_middle))


def turn_kernel(volume_ref, field_ref, edges_ref, ordered):
    rows, slices, columns = volume_ref.shape
    blocks, _, _, width = field_ref.shape
    blocks = blocks - 2

    def order(index, carry):
        at = pl.multiple_of(index * slices, slices)
        ordered[:, pl.ds(at, slices), :] = jnp.swapaxes(volume_ref[pl.ds(at, slices)], 0, 1)
        return carry

    lax.fori_loop(0, rows // slices, order, 0, unroll=2)
    field_ref[0] = jnp.zeros((slices, columns, width), jnp.float32)
    field_ref[blocks + 1] = jnp.zeros((slices, columns, width), jnp.float32)

    def turn(z, carry):
        for block in range(blocks):
            field_ref[block + 1, z] = ordered[z, block * width:(block + 1) * width, :].T.astype(jnp.float32)
        return carry

    lax.fori_loop(0, slices, turn, 0)
    for side, x in enumerate((0, columns - 1)):
        for block in range(blocks):
            edges_ref[side, :, block * width:(block + 1) * width] = field_ref[block + 1, :, x, :].astype(edges_ref.dtype)


def print_kernel(views, total_z, shift, counts_ref, numbers_ref, field_ref, left_ref, right_ref, own_ref, over_ref, *sums):
    _, slices, columns, width = field_ref.shape
    group = 8
    quad = columns // (2 * slices)
    count = columns // group
    block = lax.rem(counts_ref[0] + shift, field_ref.shape[0] - 2)
    scale = counts_ref[1].astype(jnp.float32) * (-2.0 / total_z)
    light = [[numbers_ref[3 * v + k] for k in range(3)] for v in range(views)]
    gain = [numbers_ref[3 * views + k] for k in range(4)]
    bias = [numbers_ref[3 * views + 4 + k] for k in range(4)]
    half_gain = [0.5 * gain[k] for k in range(3)]
    half_bias = [0.5 * bias[k] for k in range(3)]
    thick_gain = gain[3] * (1.0 / LN2)
    thick_bias = bias[3] * (1.0 / LN2)
    offsets = []
    slants = []
    for v in range(views):
        parts = [jnp.full((group, width), light[v][k], jnp.float32) for k in range(3)]
        square = jnp.maximum(parts[0] * parts[0] + parts[1] * parts[1] + parts[2] * parts[2], 1e-30)
        offsets.append(4.0 / square)
        unit = (0.35 * LN2) * lax.rsqrt(square)
        slants.append([part * unit for part in parts])
    line = lax.broadcasted_iota(jnp.int32, (group, width), 0)
    lane = lax.broadcasted_iota(jnp.int32, (group, width), 1)
    start = lane == 0
    end = lane == width - 1
    for part in sums:
        part[...] = jnp.zeros(part.shape, jnp.float32)
    along = pl.ds(pl.multiple_of(block * width, width), width)
    left = left_ref[:, along].astype(jnp.float32)
    right = right_ref[:, along].astype(jnp.float32)

    def work(j):
        base = j * group if isinstance(j, int) else pl.multiple_of(j * group, group)
        here_rows = pl.ds(base, group)
        fields = [field_ref[block + 1, z, here_rows, :] for z in range(slices)]
        for z in range(slices):
            here = fields[z]
            if isinstance(j, int) and j == 0:
                less = jnp.where(line == 0, left[z:z + 1, :], pltpu.roll(here, 1, 0))
            else:
                less = field_ref[block + 1, z, pl.ds(base - 1, group), :]
            if isinstance(j, int) and j == count - 1:
                more = jnp.where(line == group - 1, right[z:z + 1, :], pltpu.roll(here, group - 1, 0))
            else:
                more = field_ref[block + 1, z, pl.ds(base + 1, group), :]
            dx = more - less
            prior = pltpu.roll(jnp.where(end, field_ref[block, z, here_rows, :], here), 1, 1)
            later = pltpu.roll(jnp.where(start, field_ref[block + 2, z, here_rows, :], here), width - 1, 1)
            dy = later - prior
            if z == 0:
                dz = fields[1]
            elif z == slices - 1:
                dz = -fields[z - 1]
            else:
                dz = fields[z + 1] - fields[z - 1]
            steep = dx * dx + dy * dy + dz * dz
            w = lax.exp2(thick_gain * here + thick_bias)
            thick = scale * jnp.where(w < 0.001, w * (1.0 / LN2 - (0.5 / LN2) * w), lax.log2(1.0 + w))
            tints = [1.0 + jnp.tanh(half_gain[k] * here + half_bias[k]) for k in range(3)]
            for v in range(views):
                place = pl.ds(base + z * (v + 1) * quad, group)
                lx, ly, lz = slants[v]
                facing = dx * lx + dy * ly + dz * lz
                shade = thick * ((-0.15 * LN2) - jnp.abs(facing) * lax.rsqrt(steep + offsets[v]))
                depth = sums[4 * v + 3][place, :]
                sums[4 * v + 3][place, :] = depth + thick
                shade = shade * lax.exp2(depth)
                for k in range(3):
                    sums[4 * v + k][place, :] = sums[4 * v + k][place, :] + tints[k] * shade

    work(count - 1)

    def inner(index, carry):
        work(count - 2 - index)
        return carry

    lax.fori_loop(0, count - 2, inner, 0)
    work(0)
    for v in range(views):
        for k in range(4):
            part = sums[4 * v + k]
            own_ref[v, k] = part[:columns, :]
            rest = part[columns:, :]
            over_ref[v, k] = encode(-rest if k == 3 else rest)


def turn_volume(volume, blocks):
    rows, slices, columns = volume.shape
    return pl.pallas_call(
        turn_kernel,
        out_shape=[jax.ShapeDtypeStruct((blocks + 2, slices, columns, rows // blocks), jnp.float32),
                   jax.ShapeDtypeStruct((2, slices, rows), volume.dtype)],
        in_specs=[vmem], out_specs=[vmem] * 2, scratch_shapes=[pltpu.VMEM((slices, rows, columns), volume.dtype)],
        compiler_params=params, name="turn_rows")(volume)


def merged(own_ref, over_ref, v):
    through = lax.exp2(own_ref[v, 3])
    parts = [own_ref[v, k] + through * decode(over_ref[v, k]) for k in range(3)]
    return parts + [decode(over_ref[v, 3]) - own_ref[v, 3]]


def merge_kernel(views, own_ref, over_ref, layer_ref):
    for v in range(views):
        for k, part in enumerate(merged(own_ref, over_ref, v)):
            layer_ref[v, k] = encode(part)


def final_kernel(views, share, shifts, counts_ref, own_ref, over_ref, *refs):
    layer_refs, image_ref = refs[:-1], refs[-1]
    groups = len(shifts) + 1
    owner = counts_ref[0]
    ids = [owner] + [lax.rem(owner + groups - shift, groups) for shift in shifts]
    for v in range(views):
        order = [counts_ref[2 + v * groups + r] for r in range(groups)]
        places = [sum(jnp.where(order[r] == one, r, 0) for r in range(groups)) for one in ids]
        layers = [merged(own_ref, over_ref, v)] + [[decode(ref[v, k]) for k in range(4)] for ref in layer_refs]
        colours = [0.0] * 3
        total = 0.0
        for g in range(groups):
            front = 0.0
            for h in range(groups):
                if h != g:
                    front = front + layers[h][3] * jnp.where(places[h] < places[g], 1.0, 0.0)
            through = lax.exp2(-front)
            colours = [colours[k] + layers[g][k] * through for k in range(3)]
            total = total + layers[g][3]
        for k, part in enumerate(colours + [1.0 - lax.exp2(-total)]):
            turned = part.T
            for t in range(turned.shape[0] // share):
                block = turned[t * share:(t + 1) * share, :]
                image_ref[t, v, k] = encode(block) if image_ref.dtype == jnp.int16 else block


def place_kernel(blocks_ref, image_ref):
    tiles, views, channels, share, columns = blocks_ref.shape
    for t in range(tiles):
        for v in range(views):
            for k in range(channels):
                block = blocks_ref[t, v, k]
                block = decode(block) if block.dtype == jnp.int16 else block
                image_ref[v, k, :, t * columns:(t + 1) * columns] = block


def prints_of(field, left, right, shift, counts, numbers, views, total_z):
    blocks, slices, columns, width = field.shape
    shape = (views, 4, columns, width)
    return pl.pallas_call(
        functools.partial(print_kernel, views, total_z, shift),
        out_shape=[jax.ShapeDtypeStruct(shape, jnp.float32), jax.ShapeDtypeStruct(shape, jnp.int16)],
        in_specs=[smem] * 2 + [vmem] * 3, out_specs=[vmem] * 2,
        scratch_shapes=[pltpu.VMEM((2 * columns, width), jnp.float32)] * (4 * views),
        cost_estimate=pl.CostEstimate(flops=100 * slices * columns * width, bytes_accessed=12 * 2**20, transcendentals=0),
        compiler_params=params, name="prints")(counts, numbers, field, left, right)


def merge_of(own, over):
    return pl.pallas_call(
        functools.partial(merge_kernel, own.shape[0]), out_shape=jax.ShapeDtypeStruct(own.shape, jnp.int16),
        in_specs=[vmem] * 2, out_specs=vmem, compiler_params=params, name="merge")(own, over)


def final_of(counts, own, over, layers, shifts, share):
    views, channels, columns, width = own.shape
    kind = jnp.int16 if share % 16 == 0 else jnp.float32
    return pl.pallas_call(
        functools.partial(final_kernel, views, share, shifts),
        out_shape=jax.ShapeDtypeStruct((width // share, views, channels, share, columns), kind),
        in_specs=[smem] + [vmem] * (2 + len(layers)), out_specs=vmem, compiler_params=params,
        name="final")(counts, own, over, *layers)


def place_of(blocks):
    tiles, views, channels, share, columns = blocks.shape
    return pl.pallas_call(
        place_kernel, out_shape=jax.ShapeDtypeStruct((views, channels, share, tiles * columns), jnp.float32),
        in_specs=[vmem], out_specs=vmem, compiler_params=params, name="place")(blocks)


def passed_along(x, axis, by):
    devices = lax.axis_size(axis)
    pairs = [(i, i + by) for i in range(devices) if 0 <= i + by < devices]
    return lax.ppermute(x, axis, pairs)


def passed_round(x, axis, by):
    devices = lax.axis_size(axis)
    return lax.ppermute(x, axis, [(i, (i + by) % devices) for i in range(devices)])


def local(volume, active, depth_order, light_vector, class_gain, class_bias):
    depth_count = lax.axis_size("depth")
    tile_count = lax.axis_size("tile")
    rows, slices, columns = volume.shape
    views = light_vector.shape[0]
    total_z = slices * depth_count
    share = rows // (depth_count * tile_count)
    numbers = jnp.concatenate([light_vector.reshape(-1), class_gain, class_bias])
    here = lax.axis_index("depth").astype(jnp.int32)
    counts = jnp.concatenate([here[None], active.reshape(-1), depth_order.reshape(-1)])
    field, edges = turn_volume(volume, depth_count)
    left = passed_along(edges[1], "tile", 1)
    right = passed_along(edges[0], "tile", -1)
    far_first = sorted(range(1, depth_count), key=lambda shift: -min(shift, depth_count - shift))
    layers = []
    for shift in far_first + [0]:
        own, over = prints_of(field, left, right, shift, counts, numbers, views, total_z)
        over = passed_along(over, "tile", 1)
        if shift:
            layers.append(passed_round(merge_of(own, over), "depth", shift))
    blocks = final_of(counts, own, over, layers, far_first, share)
    blocks = lax.all_to_all(blocks, "tile", split_axis=0, concat_axis=0, tiled=True)
    return place_of(blocks)


def solution(mesh):
    placed = (P(None, "depth", "tile"), P("depth", "tile"), P(), P(), P(), P())
    return jax.shard_map(
        local,
        mesh=mesh,
        in_specs=placed,
        out_specs=P(None, None, ("depth", "tile"), None),
        check_vma=False,
    )
```

```python
import functools
import math
import jax
import jax.numpy as jnp
from jax import lax
from jax.experimental import pallas as pl
from jax.experimental.pallas import tpu as pltpu
from jax.sharding import PartitionSpec as P

LN2 = math.log(2.0)
code_step = 1638.0
code_middle = 16.0
code_none = -32768.0

smem = pl.BlockSpec(memory_space=pltpu.SMEM)
vmem = pl.BlockSpec(memory_space=pltpu.VMEM)
far = pl.BlockSpec(memory_space=pl.ANY)
small_cost = pl.CostEstimate(flops=10**10, bytes_accessed=10**8, transcendentals=0)
params = pltpu.CompilerParams(vmem_limit_bytes=12 * 1024 * 1024)
turn_params = pltpu.CompilerParams(vmem_limit_bytes=12 * 1024 * 1024)


def encode(x):
    return jnp.round(jnp.maximum(code_step * lax.log2(x) + code_step * code_middle, code_none)).astype(jnp.int16)


def decode(q):
    value = q.astype(jnp.int32).astype(jnp.float32)
    return jnp.where(value == code_none, 0.0, lax.exp2(value * (1.0 / code_step) - code_middle))


def turn_kernel(volume_ref, field_ref, low_ref, high_ref, brick, ordered, arrived):
    rows, slices, columns = volume_ref.shape
    blocks, _, _, width = field_ref.shape
    blocks = blocks - 2
    copies = []
    for block in range(blocks):
        part = pl.ds(block * width, width)
        copies.append(pltpu.make_async_copy(volume_ref.at[part], brick.at[part], arrived.at[block]))
    for copy in copies:
        copy.start()
    field_ref[0] = jnp.zeros((slices, columns, width), jnp.float32)
    field_ref[blocks + 1] = jnp.zeros((slices, columns, width), jnp.float32)
    for block in range(blocks):
        copies[block].wait()

        def order(index, carry):
            at = pl.multiple_of(block * width + index * slices, slices)
            ordered[:, pl.ds(at, slices), :] = jnp.swapaxes(brick[pl.ds(at, slices)], 0, 1)
            return carry

        lax.fori_loop(0, width // slices, order, 0, unroll=2)

        def turn(z, carry):
            field_ref[block + 1, z] = ordered[z, block * width:(block + 1) * width, :].T.astype(jnp.float32)
            return carry

        lax.fori_loop(0, slices, turn, 0, unroll=2)
        for edge_ref, x in ((low_ref, 0), (high_ref, columns - 1)):
            edge_ref[:, block * width:(block + 1) * width] = field_ref[block + 1, :, x, :].astype(edge_ref.dtype)


def make_table(total_z, active_ref, light_ref, gain_ref, bias_ref, table_ref):
    def spread(value):
        return jnp.full(table_ref.shape[1:], value, jnp.float32)

    values = [spread(active_ref[0, 0].astype(jnp.float32) * (-2.0 / total_z))]
    values += [spread(0.5 * gain_ref[k]) for k in range(3)] + [spread(gain_ref[3] * (1.0 / LN2))]
    values += [spread(0.5 * bias_ref[k]) for k in range(3)] + [spread(bias_ref[3] * (1.0 / LN2))]
    for v in range(light_ref.shape[0]):
        parts = [spread(light_ref[v, k]) for k in range(3)]
        square = jnp.maximum(parts[0] * parts[0] + parts[1] * parts[1] + parts[2] * parts[2], 1e-30)
        unit = (0.35 * LN2) * lax.rsqrt(square)
        values += [part * unit for part in parts] + [4.0 / square]
    for index, value in enumerate(values):
        table_ref[index] = value


def matter_kernel(shifts, field_ref, table_ref, thick_ref, tints_ref, slope_ref):
    _, slices, columns, width = thick_ref.shape
    group = table_ref.shape[1]
    scale = table_ref[0]
    gain = [table_ref[1 + k] for k in range(4)]
    bias = [table_ref[5 + k] for k in range(4)]
    lane = lax.broadcasted_iota(jnp.int32, (group, width), 1)
    start = lane == 0
    end = lane == width - 1
    deep = 2
    places = [(part, at * group) for part in range(deep) for at in range(columns // group)]
    for index, shift in enumerate(shifts):
        block = lax.rem(lax.axis_index("depth") + shift, field_ref.shape[0] - 2)

        def work(step, carry):
            z = step * deep
            heres = [field_ref[block + 1, z + part, at:at + group, :] for part, at in places]
            priors = [field_ref[block, z + part, at:at + group, :] for part, at in places]
            laters = [field_ref[block + 2, z + part, at:at + group, :] for part, at in places]
            done = []
            for here, prior, later in zip(heres, priors, laters):
                w = lax.exp2(gain[3] * here + bias[3])
                thick = scale * jnp.where(w < 0.001, w * (1.0 / LN2 - (0.5 / LN2) * w), lax.log2(1.0 + w))
                tints = [1.0 + jnp.tanh(gain[k] * here + bias[k]) for k in range(3)]
                prior = pltpu.roll(jnp.where(end, prior, here), 1, 1)
                later = pltpu.roll(jnp.where(start, later, here), width - 1, 1)
                done.append((thick, tints, later - prior))
            for (part, at), (thick, tints, slope) in zip(places, done):
                thick_ref[index, z + part, at:at + group, :] = thick
                for k in range(3):
                    tints_ref[index, k, z + part, at:at + group, :] = tints[k]
                slope_ref[index, z + part, at:at + group, :] = slope
            return carry

        lax.fori_loop(0, slices // deep, work, 0)


def first_matter_kernel(shifts, total_z, active_ref, light_ref, gain_ref, bias_ref, field_ref, table_ref, *refs):
    make_table(total_z, active_ref, light_ref, gain_ref, bias_ref, table_ref)
    matter_kernel(shifts, field_ref, table_ref, *refs)


def print_kernel(parts, matters, field_ref, table_ref, left_ref, right_ref, after_ref, *refs):
    matter_refs, own_ref, over_ref, sums = refs[:3 * matters], refs[3 * matters], refs[3 * matters + 1], refs[3 * matters + 2:]
    for index, (shift, source, place) in enumerate(parts):
        chosen = [ref.at[place] for ref in matter_refs[3 * source:3 * source + 3]]
        print_chunk(shift, field_ref, table_ref, left_ref, right_ref, *chosen, own_ref.at[index], over_ref.at[index], *sums)


def print_chunk(shift, field_ref, table_ref, left_ref, right_ref, thick_ref, tints_ref, slope_ref, own_ref, over_ref, *sums):
    blocks, slices, columns, width = field_ref.shape
    group = table_ref.shape[1]
    views = own_ref.shape[0]
    quad = columns // (2 * slices)
    count = columns // group
    block = lax.rem(lax.axis_index("depth") + shift, blocks - 2)
    slants = [[table_ref[9 + 4 * v + k] for k in range(3)] for v in range(views)]
    offsets = [table_ref[12 + 4 * v] for v in range(views)]
    line = lax.broadcasted_iota(jnp.int32, (group, width), 0)
    for part in sums:
        part[...] = jnp.zeros(part.shape, jnp.float32)
    along = pl.ds(pl.multiple_of(block * width, width), width)
    left = left_ref[:, along].astype(jnp.float32)
    right = right_ref[:, along].astype(jnp.float32)

    def work(j):
        base = j * group if isinstance(j, int) else pl.multiple_of(j * group, group)
        here_rows = pl.ds(base, group)
        for z in range(slices):
            if isinstance(j, int) and j == 0:
                less = jnp.where(line == 0, left[z:z + 1, :], pltpu.roll(field_ref[block + 1, z, here_rows, :], 1, 0))
            else:
                less = field_ref[block + 1, z, pl.ds(base - 1, group), :]
            if isinstance(j, int) and j == count - 1:
                more = jnp.where(line == group - 1, right[z:z + 1, :],
                                 pltpu.roll(field_ref[block + 1, z, here_rows, :], group - 1, 0))
            else:
                more = field_ref[block + 1, z, pl.ds(base + 1, group), :]
            dx = more - less
            dy = slope_ref[z, here_rows, :]
            if z == 0:
                dz = field_ref[block + 1, z + 1, here_rows, :]
            elif z == slices - 1:
                dz = -field_ref[block + 1, z - 1, here_rows, :]
            else:
                dz = field_ref[block + 1, z + 1, here_rows, :] - field_ref[block + 1, z - 1, here_rows, :]
            steep = dx * dx + dy * dy + dz * dz
            thick = thick_ref[z, here_rows, :]
            tints = [tints_ref[k, z, here_rows, :] for k in range(3)]
            for v in range(views):
                place = pl.ds(base + z * (v + 1) * quad, group)
                lx, ly, lz = slants[v]
                facing = dx * lx + dy * ly + dz * lz
                shade = thick * ((-0.15 * LN2) - jnp.abs(facing) * lax.rsqrt(steep + offsets[v]))
                depth = sums[4 * v + 3][place, :]
                sums[4 * v + 3][place, :] = depth + thick
                shade = shade * lax.exp2(depth)
                for k in range(3):
                    sums[4 * v + k][place, :] = sums[4 * v + k][place, :] + tints[k] * shade

    work(count - 1)

    def inner(index, carry):
        work(count - 2 - index)
        return carry

    lax.fori_loop(0, count - 2, inner, 0)
    work(0)
    for v in range(views):
        for k in range(4):
            part = sums[4 * v + k]
            own_ref[v, k] = part[:columns, :]
            first, count = over_rows(v, slices, columns)
            rest = part[columns:columns + count, :]
            over_ref[k, first:first + count, :] = encode(-rest if k == 3 else rest)


def over_rows(v, slices, columns):
    quad = columns // (2 * slices)
    ends = [-(-(slices - 1) * (view + 1) * quad // 16) * 16 for view in range(v + 1)]
    return sum(ends[:-1]), ends[-1]


def merged(own_ref, over_ref, v, slices):
    first, count = over_rows(v, slices, own_ref.shape[2])
    through = lax.exp2(own_ref[v, 3, :count, :])
    overs = [decode(over_ref[k, first:first + count, :]) for k in range(4)]
    tops = [own_ref[v, k, :count, :] + through * overs[k] for k in range(3)] + [overs[3] - own_ref[v, 3, :count, :]]
    if count == own_ref.shape[2]:
        return tops
    lows = [own_ref[v, k, count:, :] * (1.0 if k < 3 else -1.0) for k in range(4)]
    return [jnp.concatenate([top, low]) for top, low in zip(tops, lows)]


def merge_kernel(slices, layers, own_ref, over_ref, later_ref, *refs):
    for index, layer_ref in enumerate(refs[:layers]):
        for v in range(own_ref.shape[1]):
            for k, part in enumerate(merged(own_ref.at[index], over_ref.at[index], v, slices)):
                layer_ref[v, k] = encode(part)
    for ref in refs[layers:]:
        ref[...] = later_ref[...]


def final_kernel(views, share, slices, shifts, order_ref, own_ref, over_ref, *refs):
    layer_refs, image_ref = refs[:-1], refs[-1]
    groups = len(shifts) + 1
    owner = lax.axis_index("depth")
    ids = [owner] + [lax.rem(owner + groups - shift, groups) for shift in shifts]
    for v in range(views):
        order = [order_ref[v, r] for r in range(groups)]
        places = [sum(jnp.where(order[r] == one, r, 0) for r in range(groups)) for one in ids]
        layers = [merged(own_ref.at[0], over_ref.at[0], v, slices)] + [[decode(ref[v, k]) for k in range(4)] for ref in layer_refs]
        colours = [0.0] * 3
        total = 0.0
        for g in range(groups):
            front = 0.0
            for h in range(groups):
                if h != g:
                    front = front + layers[h][3] * jnp.where(places[h] < places[g], 1.0, 0.0)
            through = lax.exp2(-front)
            colours = [colours[k] + layers[g][k] * through for k in range(3)]
            total = total + layers[g][3]
        for k, part in enumerate(colours + [1.0 - lax.exp2(-total)]):
            turned = part.T
            for t in range(turned.shape[0] // share):
                block = turned[t * share:(t + 1) * share, :]
                image_ref[t, v, k] = encode(block) if image_ref.dtype == jnp.int16 else block


def place_kernel(blocks_ref, image_ref):
    tiles, views, channels, share, columns = blocks_ref.shape
    for t in range(tiles):
        for v in range(views):
            for k in range(channels):
                block = blocks_ref[t, v, k]
                block = decode(block) if block.dtype == jnp.int16 else block
                image_ref[v, k, :, t * columns:(t + 1) * columns] = block


def turn_volume(volume, blocks):
    rows, slices, columns = volume.shape
    width = rows // blocks
    edge = jax.ShapeDtypeStruct((slices, rows), volume.dtype)
    return pl.pallas_call(
        turn_kernel,
        out_shape=[jax.ShapeDtypeStruct((blocks + 2, slices, columns, width), jnp.float32), edge, edge],
        in_specs=[far], out_specs=[vmem] * 3,
        scratch_shapes=[pltpu.VMEM(volume.shape, volume.dtype), pltpu.VMEM((slices, rows, columns), volume.dtype),
                        pltpu.SemaphoreType.DMA((blocks,))],
        cost_estimate=pl.CostEstimate(flops=1, bytes_accessed=16 * 1024 * 1024, transcendentals=0),
        compiler_params=turn_params, name="turn_rows")(volume)


def matter_of(field, shifts, table=None, smalls=(), after=()):
    blocks, slices, columns, width = field.shape
    shape = (len(shifts), slices, columns, width)
    outs = [jax.ShapeDtypeStruct(shape, jnp.float32), jax.ShapeDtypeStruct((len(shifts), 3) + shape[1:], jnp.float32),
            jax.ShapeDtypeStruct(shape, jnp.float32)]
    if table is not None:
        return pl.pallas_call(
            functools.partial(matter_kernel, shifts), out_shape=outs, in_specs=[vmem] * 2, out_specs=[vmem] * 3,
            cost_estimate=small_cost, compiler_params=params, name="matter")(field, table)
    table = jax.ShapeDtypeStruct((9 + 4 * smalls[1].shape[0], 8, width), jnp.float32)
    return pl.pallas_call(
        functools.partial(first_matter_kernel, shifts, slices * (blocks - 2)), out_shape=[table] + outs,
        in_specs=[smem] * 4 + [vmem], out_specs=[vmem] * 4,
        cost_estimate=small_cost, compiler_params=params, name="matter")(*smalls, field)


def prints_of(field, matters, table, left, right, after, parts, views):
    blocks, slices, columns, width = field.shape
    shape = (len(parts), views, 4, columns, width)
    over_shape = (len(parts), 4, sum(over_rows(views - 1, slices, columns)), width)
    arrays = [array for matter in matters for array in matter]
    return pl.pallas_call(
        functools.partial(print_kernel, parts, len(matters)),
        out_shape=[jax.ShapeDtypeStruct(shape, jnp.float32), jax.ShapeDtypeStruct(over_shape, jnp.int16)],
        in_specs=[vmem] * 4 + [far] + [vmem] * len(arrays), out_specs=[vmem] * 2,
        scratch_shapes=[pltpu.VMEM((2 * columns, width), jnp.float32)] * (4 * views),
        cost_estimate=small_cost, compiler_params=params, name="prints")(field, table, left, right, after, *arrays)


def merge_of(own, over, later, slices, pass_later):
    layers = own.shape[0]
    outs = [jax.ShapeDtypeStruct(own.shape[1:], jnp.int16)] * layers
    outs += [jax.ShapeDtypeStruct(later.shape, later.dtype)] * pass_later
    return pl.pallas_call(
        functools.partial(merge_kernel, slices, layers), out_shape=outs,
        in_specs=[vmem] * 2 + [vmem if pass_later else far], out_specs=[vmem] * len(outs), cost_estimate=small_cost,
        compiler_params=params, name="merge")(own, over, later)


def final_of(depth_order, own, over, layers, shifts, share, slices):
    _, views, channels, columns, width = own.shape
    kind = jnp.int16 if share % 16 == 0 else jnp.float32
    return pl.pallas_call(
        functools.partial(final_kernel, views, share, slices, shifts),
        out_shape=jax.ShapeDtypeStruct((width // share, views, channels, share, columns), kind),
        in_specs=[smem] + [vmem] * (2 + len(layers)), out_specs=vmem, compiler_params=params,
        name="final")(depth_order, own, over, *layers)


def place_of(blocks):
    tiles, views, channels, share, columns = blocks.shape
    return pl.pallas_call(
        place_kernel, out_shape=jax.ShapeDtypeStruct((views, channels, share, tiles * columns), jnp.float32),
        in_specs=[vmem], out_specs=vmem, compiler_params=params, name="place")(blocks)


def passed_along(x, axis, by):
    devices = lax.axis_size(axis)
    pairs = [(i, i + by) for i in range(devices) if 0 <= i + by < devices]
    return lax.ppermute(x, axis, pairs)


def passed_round(x, axis, by):
    devices = lax.axis_size(axis)
    return lax.ppermute(x, axis, [(i, (i + by) % devices) for i in range(devices)])


def local(volume, active, depth_order, light_vector, class_gain, class_bias):
    depth_count = lax.axis_size("depth")
    tile_count = lax.axis_size("tile")
    rows, slices, columns = volume.shape
    share = rows // (depth_count * tile_count)
    field, low, high = turn_volume(volume, depth_count)
    left = passed_along(high, "tile", 1)
    right = passed_along(low, "tile", -1)
    shifts = sorted(range(1, depth_count), key=lambda shift: -min(shift, depth_count - shift)) + [0]
    half = (len(shifts) + 1) // 2
    table, *early = matter_of(field, shifts[:half], smalls=(active, light_vector, class_gain, class_bias))
    late = matter_of(field, shifts[half:], table=table)
    sources = [(shift, index // half, index % half) for index, shift in enumerate(shifts)]

    def chunks(parts, after):
        return prints_of(field, (early, late) if any(part[1] for part in parts) else (early,), table, left, right, after,
                         parts, light_vector.shape[0])

    own, over = chunks(sources[:1], left)
    layer, = merge_of(own, passed_along(over, "tile", 1), left, slices, 0)
    layers = [passed_round(layer, "depth", shifts[0])]
    middle, middle_over = chunks(sources[1:-1], layer)
    last, last_over = chunks(sources[-1:], middle)
    *middle_layers, last_over = merge_of(middle, passed_along(middle_over, "tile", 1), last_over, slices, 1)
    last_over = passed_along(last_over, "tile", 1)
    layers += [passed_round(layer, "depth", shift) for layer, shift in zip(middle_layers, shifts[1:-1])]
    blocks = final_of(depth_order, last, last_over, layers, shifts[:-1], share, slices)
    blocks = lax.all_to_all(blocks, "tile", split_axis=0, concat_axis=0, tiled=True)
    return place_of(blocks)


def solution(mesh):
    placed = (P(None, "depth", "tile"), P("depth", "tile"), P(), P(), P(), P())
    return jax.shard_map(
        local,
        mesh=mesh,
        in_specs=placed,
        out_specs=P(None, None, ("depth", "tile"), None),
        check_vma=False,
    )
```

```python
import functools
import math
import jax
import jax.numpy as jnp
from jax import lax
from jax.experimental import pallas as pl
from jax.experimental.pallas import tpu as pltpu
from jax.sharding import PartitionSpec as P

LN2 = math.log(2.0)
code_step = 1638.0
code_middle = 16.0
code_none = -32768.0

smem = pl.BlockSpec(memory_space=pltpu.SMEM)
vmem = pl.BlockSpec(memory_space=pltpu.VMEM)
far = pl.BlockSpec(memory_space=pl.ANY)
small_cost = pl.CostEstimate(flops=10**10, bytes_accessed=10**8, transcendentals=0)
params = pltpu.CompilerParams(vmem_limit_bytes=12 * 1024 * 1024)
turn_params = pltpu.CompilerParams(vmem_limit_bytes=12 * 1024 * 1024)


def encode(x):
    return jnp.round(jnp.maximum(code_step * lax.log2(x) + code_step * code_middle, code_none)).astype(jnp.int16)


def decode(q):
    value = q.astype(jnp.int32).astype(jnp.float32)
    return jnp.where(value == code_none, 0.0, lax.exp2(value * (1.0 / code_step) - code_middle))


def turn_kernel(volume_ref, field_ref, low_ref, high_ref, ordered):
    rows, slices, columns = volume_ref.shape
    blocks, _, _, width = field_ref.shape
    blocks = blocks - 2

    def order(index, carry):
        at = pl.multiple_of(index * slices, slices)
        ordered[:, pl.ds(at, slices), :] = jnp.swapaxes(volume_ref[pl.ds(at, slices)], 0, 1)
        return carry

    lax.fori_loop(0, rows // slices, order, 0, unroll=4)
    field_ref[0] = jnp.zeros((slices, columns, width), jnp.float32)
    field_ref[blocks + 1] = jnp.zeros((slices, columns, width), jnp.float32)

    def turn(z, carry):
        for block in range(blocks):
            field_ref[block + 1, z] = ordered[z, block * width:(block + 1) * width, :].T.astype(jnp.float32)
        return carry

    lax.fori_loop(0, slices, turn, 0)
    for edge_ref, x in ((low_ref, 0), (high_ref, columns - 1)):
        for block in range(blocks):
            edge_ref[:, block * width:(block + 1) * width] = field_ref[block + 1, :, x, :].astype(edge_ref.dtype)


def make_table(total_z, active_ref, light_ref, gain_ref, bias_ref, table_ref):
    def spread(value):
        return jnp.full(table_ref.shape[1:], value, jnp.float32)

    values = [spread(active_ref[0, 0].astype(jnp.float32) * (-2.0 / total_z))]
    values += [spread(0.5 * gain_ref[k]) for k in range(3)] + [spread(gain_ref[3] * (1.0 / LN2))]
    values += [spread(0.5 * bias_ref[k]) for k in range(3)] + [spread(bias_ref[3] * (1.0 / LN2))]
    for v in range(light_ref.shape[0]):
        parts = [spread(light_ref[v, k]) for k in range(3)]
        square = jnp.maximum(parts[0] * parts[0] + parts[1] * parts[1] + parts[2] * parts[2], 1e-30)
        unit = (0.35 * LN2) * lax.rsqrt(square)
        values += [part * unit for part in parts] + [4.0 / square]
    for index, value in enumerate(values):
        table_ref[index] = value


def matter_kernel(shifts, field_ref, table_ref, after_ref, thick_ref, tints_ref, slope_ref):
    _, slices, columns, width = thick_ref.shape
    group = table_ref.shape[1]
    scale = table_ref[0]
    gain = [table_ref[1 + k] for k in range(4)]
    bias = [table_ref[5 + k] for k in range(4)]
    lane = lax.broadcasted_iota(jnp.int32, (group, width), 1)
    start = lane == 0
    end = lane == width - 1
    deep = 2
    places = [(part, at * group) for part in range(deep) for at in range(columns // group)]
    for index, shift in enumerate(shifts):
        block = lax.rem(lax.axis_index("depth") + shift, field_ref.shape[0] - 2)

        def work(step, carry):
            z = step * deep
            heres = [field_ref[block + 1, z + part, at:at + group, :] for part, at in places]
            priors = [field_ref[block, z + part, at:at + group, :] for part, at in places]
            laters = [field_ref[block + 2, z + part, at:at + group, :] for part, at in places]
            done = []
            for here, prior, later in zip(heres, priors, laters):
                w = lax.exp2(gain[3] * here + bias[3])
                thick = scale * jnp.where(w < 0.001, w * (1.0 / LN2 - (0.5 / LN2) * w), lax.log2(1.0 + w))
                tints = [1.0 + jnp.tanh(gain[k] * here + bias[k]) for k in range(3)]
                prior = pltpu.roll(jnp.where(end, prior, here), 1, 1)
                later = pltpu.roll(jnp.where(start, later, here), width - 1, 1)
                done.append((thick, tints, later - prior))
            for (part, at), (thick, tints, slope) in zip(places, done):
                thick_ref[index, z + part, at:at + group, :] = thick
                for k in range(3):
                    tints_ref[index, k, z + part, at:at + group, :] = tints[k]
                slope_ref[index, z + part, at:at + group, :] = slope
            return carry

        lax.fori_loop(0, slices // deep, work, 0)


def first_matter_kernel(shifts, total_z, active_ref, light_ref, gain_ref, bias_ref, field_ref, table_ref, *refs):
    make_table(total_z, active_ref, light_ref, gain_ref, bias_ref, table_ref)
    matter_kernel(shifts, field_ref, table_ref, None, *refs)


def print_kernel(parts, matters, field_ref, table_ref, left_ref, right_ref, after_ref, *refs):
    matter_refs, own_ref, over_ref, sums = refs[:3 * matters], refs[3 * matters], refs[3 * matters + 1], refs[3 * matters + 2:]
    for index, (shift, source, place) in enumerate(parts):
        chosen = [ref.at[place] for ref in matter_refs[3 * source:3 * source + 3]]
        print_chunk(shift, field_ref, table_ref, left_ref, right_ref, *chosen, own_ref.at[index], over_ref.at[index], *sums)


def print_chunk(shift, field_ref, table_ref, left_ref, right_ref, thick_ref, tints_ref, slope_ref, own_ref, over_ref, *sums):
    blocks, slices, columns, width = field_ref.shape
    group = table_ref.shape[1]
    views = own_ref.shape[0]
    quad = columns // (2 * slices)
    count = columns // group
    block = lax.rem(lax.axis_index("depth") + shift, blocks - 2)
    slants = [[table_ref[9 + 4 * v + k] for k in range(3)] for v in range(views)]
    offsets = [table_ref[12 + 4 * v] for v in range(views)]
    line = lax.broadcasted_iota(jnp.int32, (group, width), 0)
    for part in sums:
        part[...] = jnp.zeros(part.shape, jnp.float32)
    along = pl.ds(pl.multiple_of(block * width, width), width)
    tile = lax.axis_index("tile")
    left = left_ref[:, along].astype(jnp.float32) * jnp.where(tile > 0, 1.0, 0.0)
    right = right_ref[:, along].astype(jnp.float32) * jnp.where(tile + 1 < lax.axis_size("tile"), 1.0, 0.0)

    def work(j):
        base = j * group if isinstance(j, int) else pl.multiple_of(j * group, group)
        here_rows = pl.ds(base, group)
        for z in range(slices):
            if isinstance(j, int) and j == 0:
                less = jnp.where(line == 0, left[z:z + 1, :], pltpu.roll(field_ref[block + 1, z, here_rows, :], 1, 0))
            else:
                less = field_ref[block + 1, z, pl.ds(base - 1, group), :]
            if isinstance(j, int) and j == count - 1:
                more = jnp.where(line == group - 1, right[z:z + 1, :],
                                 pltpu.roll(field_ref[block + 1, z, here_rows, :], group - 1, 0))
            else:
                more = field_ref[block + 1, z, pl.ds(base + 1, group), :]
            dx = more - less
            dy = slope_ref[z, here_rows, :]
            if z == 0:
                dz = field_ref[block + 1, z + 1, here_rows, :]
            elif z == slices - 1:
                dz = -field_ref[block + 1, z - 1, here_rows, :]
            else:
                dz = field_ref[block + 1, z + 1, here_rows, :] - field_ref[block + 1, z - 1, here_rows, :]
            steep = dx * dx + dy * dy + dz * dz
            thick = thick_ref[z, here_rows, :]
            tints = [tints_ref[k, z, here_rows, :] for k in range(3)]
            for v in range(views):
                place = pl.ds(base + z * (v + 1) * quad, group)
                lx, ly, lz = slants[v]
                facing = dx * lx + dy * ly + dz * lz
                shade = thick * ((-0.15 * LN2) - jnp.abs(facing) * lax.rsqrt(steep + offsets[v]))
                depth = sums[4 * v + 3][place, :]
                sums[4 * v + 3][place, :] = depth + thick
                shade = shade * lax.exp2(depth)
                for k in range(3):
                    sums[4 * v + k][place, :] = sums[4 * v + k][place, :] + tints[k] * shade

    work(count - 1)

    def inner(index, carry):
        work(count - 2 - index)
        return carry

    lax.fori_loop(0, count - 2, inner, 0)
    work(0)
    for v in range(views):
        for k in range(4):
            part = sums[4 * v + k]
            own_ref[v, k] = part[:columns, :]
            first, count = over_rows(v, slices, columns)
            rest = part[columns:columns + count, :]
            over_ref[k, first:first + count, :] = encode(-rest if k == 3 else rest)


def over_rows(v, slices, columns):
    quad = columns // (2 * slices)
    ends = [-(-(slices - 1) * (view + 1) * quad // 16) * 16 for view in range(v + 1)]
    return sum(ends[:-1]), ends[-1]


def merged(own_ref, over_ref, v, slices):
    first, count = over_rows(v, slices, own_ref.shape[2])
    through = lax.exp2(own_ref[v, 3, :count, :])
    inside = jnp.where(lax.axis_index("tile") > 0, 1.0, 0.0)
    overs = [decode(over_ref[k, first:first + count, :]) * inside for k in range(4)]
    tops = [own_ref[v, k, :count, :] + through * overs[k] for k in range(3)] + [overs[3] - own_ref[v, 3, :count, :]]
    if count == own_ref.shape[2]:
        return tops
    lows = [own_ref[v, k, count:, :] * (1.0 if k < 3 else -1.0) for k in range(4)]
    return [jnp.concatenate([top, low]) for top, low in zip(tops, lows)]


def merge_kernel(slices, layers, own_ref, over_ref, later_ref, *refs):
    for index, layer_ref in enumerate(refs[:layers]):
        for v in range(own_ref.shape[1]):
            for k, part in enumerate(merged(own_ref.at[index], over_ref.at[index], v, slices)):
                layer_ref[v, k] = encode(part)
    for ref in refs[layers:]:
        ref[...] = later_ref[...]


def final_kernel(views, share, slices, shifts, order_ref, own_ref, over_ref, *refs):
    layer_refs, image_ref = refs[:-1], refs[-1]
    groups = len(shifts) + 1
    owner = lax.axis_index("depth")
    ids = [owner] + [lax.rem(owner + groups - shift, groups) for shift in shifts]
    for v in range(views):
        order = [order_ref[v, r] for r in range(groups)]
        places = [sum(jnp.where(order[r] == one, r, 0) for r in range(groups)) for one in ids]
        layers = [merged(own_ref.at[0], over_ref.at[0], v, slices)] + [[decode(ref[v, k]) for k in range(4)] for ref in layer_refs]
        colours = [0.0] * 3
        total = 0.0
        for g in range(groups):
            front = 0.0
            for h in range(groups):
                if h != g:
                    front = front + layers[h][3] * jnp.where(places[h] < places[g], 1.0, 0.0)
            through = lax.exp2(-front)
            colours = [colours[k] + layers[g][k] * through for k in range(3)]
            total = total + layers[g][3]
        for k, part in enumerate(colours + [1.0 - lax.exp2(-total)]):
            turned = part.T
            for t in range(turned.shape[0] // share):
                block = turned[t * share:(t + 1) * share, :]
                image_ref[t, v, k] = encode(block) if image_ref.dtype == jnp.int16 else block


def place_kernel(blocks_ref, image_ref):
    tiles, views, channels, share, columns = blocks_ref.shape
    for t in range(tiles):
        for v in range(views):
            for k in range(channels):
                block = blocks_ref[t, v, k]
                block = decode(block) if block.dtype == jnp.int16 else block
                image_ref[v, k, :, t * columns:(t + 1) * columns] = block


def turn_volume(volume, blocks):
    rows, slices, columns = volume.shape
    width = rows // blocks
    edge = jax.ShapeDtypeStruct((slices, rows), volume.dtype)
    return pl.pallas_call(
        turn_kernel,
        out_shape=[jax.ShapeDtypeStruct((blocks + 2, slices, columns, width), jnp.float32), edge, edge],
        in_specs=[vmem], out_specs=[vmem] * 3, scratch_shapes=[pltpu.VMEM((slices, rows, columns), volume.dtype)],
        cost_estimate=pl.CostEstimate(flops=1, bytes_accessed=16 * 1024 * 1024, transcendentals=0),
        compiler_params=turn_params, name="turn_rows")(volume)


def matter_of(field, shifts, table=None, smalls=(), after=None):
    blocks, slices, columns, width = field.shape
    shape = (len(shifts), slices, columns, width)
    outs = [jax.ShapeDtypeStruct(shape, jnp.float32), jax.ShapeDtypeStruct((len(shifts), 3) + shape[1:], jnp.float32),
            jax.ShapeDtypeStruct(shape, jnp.float32)]
    if table is not None:
        return pl.pallas_call(
            functools.partial(matter_kernel, shifts), out_shape=outs, in_specs=[vmem] * 2 + [far], out_specs=[vmem] * 3,
            cost_estimate=small_cost, compiler_params=params, name="matter")(field, table, after)
    table = jax.ShapeDtypeStruct((9 + 4 * smalls[1].shape[0], 8, width), jnp.float32)
    return pl.pallas_call(
        functools.partial(first_matter_kernel, shifts, slices * (blocks - 2)), out_shape=[table] + outs,
        in_specs=[smem] * 4 + [vmem], out_specs=[vmem] * 4,
        cost_estimate=small_cost, compiler_params=params, name="matter")(*smalls, field)


def prints_of(field, matters, table, left, right, after, parts, views):
    blocks, slices, columns, width = field.shape
    shape = (len(parts), views, 4, columns, width)
    over_shape = (len(parts), 4, sum(over_rows(views - 1, slices, columns)), width)
    arrays = [array for matter in matters for array in matter]
    return pl.pallas_call(
        functools.partial(print_kernel, parts, len(matters)),
        out_shape=[jax.ShapeDtypeStruct(shape, jnp.float32), jax.ShapeDtypeStruct(over_shape, jnp.int16)],
        in_specs=[vmem] * 4 + [far] + [vmem] * len(arrays), out_specs=[vmem] * 2,
        scratch_shapes=[pltpu.VMEM((2 * columns, width), jnp.float32)] * (4 * views),
        cost_estimate=small_cost, compiler_params=params, name="prints")(field, table, left, right, after, *arrays)


def merge_of(own, over, later, slices, pass_later):
    layers = own.shape[0]
    outs = [jax.ShapeDtypeStruct(own.shape[1:], jnp.int16)] * layers
    outs += [jax.ShapeDtypeStruct(later.shape, later.dtype)] * pass_later
    return pl.pallas_call(
        functools.partial(merge_kernel, slices, layers), out_shape=outs,
        in_specs=[vmem] * 2 + [vmem if pass_later else far], out_specs=[vmem] * len(outs), cost_estimate=small_cost,
        compiler_params=params, name="merge")(own, over, later)


def final_of(depth_order, own, over, layers, shifts, share, slices):
    _, views, channels, columns, width = own.shape
    kind = jnp.int16 if share % 16 == 0 else jnp.float32
    return pl.pallas_call(
        functools.partial(final_kernel, views, share, slices, shifts),
        out_shape=jax.ShapeDtypeStruct((width // share, views, channels, share, columns), kind),
        in_specs=[smem] + [vmem] * (2 + len(layers)), out_specs=vmem, compiler_params=params,
        name="final")(depth_order, own, over, *layers)


def place_of(blocks):
    tiles, views, channels, share, columns = blocks.shape
    return pl.pallas_call(
        place_kernel, out_shape=jax.ShapeDtypeStruct((views, channels, share, tiles * columns), jnp.float32),
        in_specs=[vmem], out_specs=vmem, compiler_params=params, name="place")(blocks)


def passed_round(x, axis, by):
    devices = lax.axis_size(axis)
    return lax.ppermute(x, axis, [(i, (i + by) % devices) for i in range(devices)])


def local(volume, active, depth_order, light_vector, class_gain, class_bias):
    depth_count = lax.axis_size("depth")
    tile_count = lax.axis_size("tile")
    rows, slices, columns = volume.shape
    share = rows // (depth_count * tile_count)
    field, low, high = turn_volume(volume, depth_count)
    left = passed_round(high, "tile", 1)
    right = passed_round(low, "tile", -1)
    shifts = sorted(range(1, depth_count), key=lambda shift: -min(shift, depth_count - shift)) + [0]
    half = (len(shifts) + 1) // 2
    table, *early = matter_of(field, shifts[:half], smalls=(active, light_vector, class_gain, class_bias))
    sources = [(shift, index // half, index % half) for index, shift in enumerate(shifts)]

    def chunk(index, after):
        matters = (early,) if index < half else (late,)
        return prints_of(field, matters, table, left, right, after, [(shifts[index], 0, index % half)], light_vector.shape[0])

    ready, waiting, layers = left, None, []
    for index in range(len(shifts)):
        if index == half:
            late = matter_of(field, shifts[half:], table=table, after=ready)
            layer, = merge_of(*waiting, late[0], slices, 0)
            layers.append(layer)
            ready, waiting = layer, None
        own, over = chunk(index, ready)
        ready = own
        if waiting is not None:
            layer, *passed = merge_of(*waiting, over, slices, int(index + 1 == len(shifts)))
            over = passed[0] if passed else over
            layers.append(layer)
            ready = layer
        waiting = own, passed_round(over, "tile", 1)
    layers = [passed_round(layer, "depth", shift) for layer, shift in zip(layers, shifts)]
    blocks = final_of(depth_order, *waiting, layers, shifts[:-1], share, slices)
    blocks = lax.all_to_all(blocks, "tile", split_axis=0, concat_axis=0, tiled=True)
    return place_of(blocks)


def solution(mesh):
    placed = (P(None, "depth", "tile"), P("depth", "tile"), P(), P(), P(), P())
    return jax.shard_map(
        local,
        mesh=mesh,
        in_specs=placed,
        out_specs=P(None, None, ("depth", "tile"), None),
        check_vma=False,
    )
```

```python
import functools
import math
import jax
import jax.numpy as jnp
from jax import lax
from jax.experimental import pallas as pl
from jax.experimental.pallas import tpu as pltpu
from jax.sharding import PartitionSpec as P

LN2 = math.log(2.0)
code_step = 1638.0
code_middle = 16.0
code_none = -32768.0

smem = pl.BlockSpec(memory_space=pltpu.SMEM)
vmem = pl.BlockSpec(memory_space=pltpu.VMEM)
far = pl.BlockSpec(memory_space=pl.ANY)
long_cost = pl.CostEstimate(flops=10**10, bytes_accessed=10**8, transcendentals=0)
short_cost = pl.CostEstimate(flops=10**8, bytes_accessed=10**6, transcendentals=0)
params = pltpu.CompilerParams(vmem_limit_bytes=12 * 1024 * 1024)
turn_params = pltpu.CompilerParams(vmem_limit_bytes=12 * 1024 * 1024)


def encode(x):
    return jnp.round(jnp.maximum(code_step * lax.log2(x) + code_step * code_middle, code_none)).astype(jnp.int16)


def decode(q):
    value = q.astype(jnp.int32).astype(jnp.float32)
    return jnp.where(value == code_none, 0.0, lax.exp2(value * (1.0 / code_step) - code_middle))


def turn_kernel(volume_ref, field_ref, low_ref, high_ref, ordered):
    rows, slices, columns = volume_ref.shape
    blocks, _, _, width = field_ref.shape
    blocks = blocks - 1

    def order(index, carry):
        at = pl.multiple_of(index * slices, slices)
        ordered[:, pl.ds(at, slices), :] = jnp.swapaxes(volume_ref[pl.ds(at, slices)], 0, 1)
        return carry

    lax.fori_loop(0, rows // slices, order, 0, unroll=4)
    field_ref[blocks] = jnp.zeros((slices, columns, width), jnp.float32)

    def turn(z, carry):
        for block in range(blocks):
            field_ref[block, z] = ordered[z, block * width:(block + 1) * width, :].T.astype(jnp.float32)
        return carry

    lax.fori_loop(0, slices, turn, 0)
    for edge_ref, x in ((low_ref, 0), (high_ref, columns - 1)):
        for block in range(blocks):
            edge_ref[:, block * width:(block + 1) * width] = field_ref[block, :, x, :].astype(edge_ref.dtype)


def make_table(total_z, active_ref, light_ref, gain_ref, bias_ref, table_ref):
    def spread(value):
        return jnp.full(table_ref.shape[1:], value, jnp.float32)

    values = [jnp.broadcast_to(active_ref[...].astype(jnp.float32) * (-2.0 / total_z), table_ref.shape[1:])]
    values += [spread(0.5 * gain_ref[k]) for k in range(3)] + [spread(gain_ref[3] * (1.0 / LN2))]
    values += [spread(0.5 * bias_ref[k]) for k in range(3)] + [spread(bias_ref[3] * (1.0 / LN2))]
    for v in range(light_ref.shape[0]):
        parts = [spread(light_ref[v, k]) for k in range(3)]
        square = jnp.maximum(parts[0] * parts[0] + parts[1] * parts[1] + parts[2] * parts[2], 1e-30)
        unit = (0.35 * LN2) * lax.rsqrt(square)
        values += [part * unit for part in parts] + [4.0 / square]
    for index, value in enumerate(values):
        table_ref[index] = value


def matter_kernel(shift, field_ref, table_ref, after_ref, thick_ref, tints_ref, slope_ref):
    slices, columns, width = thick_ref.shape
    group = table_ref.shape[1]
    scale = table_ref[0]
    gain = [table_ref[1 + k] for k in range(4)]
    bias = [table_ref[5 + k] for k in range(4)]
    lane = lax.broadcasted_iota(jnp.int32, (group, width), 1)
    start = lane == 0
    end = lane == width - 1
    deep = 2
    places = [(part, at * group) for part in range(deep) for at in range(columns // group)]
    blocks = field_ref.shape[0] - 1
    block = lax.rem(lax.axis_index("depth") + shift, blocks)
    before = jnp.where(block == 0, blocks, block - 1)
    behind = block + 1

    def work(step, carry):
        z = step * deep
        heres = [field_ref[block, z + part, at:at + group, :] for part, at in places]
        priors = [field_ref[before, z + part, at:at + group, :] for part, at in places]
        laters = [field_ref[behind, z + part, at:at + group, :] for part, at in places]
        done = []
        for here, prior, later in zip(heres, priors, laters):
            w = lax.exp2(gain[3] * here + bias[3])
            thick = scale * jnp.where(w < 0.001, w * (1.0 / LN2 - (0.5 / LN2) * w), lax.log2(1.0 + w))
            tints = [1.0 + jnp.tanh(gain[k] * here + bias[k]) for k in range(3)]
            prior = pltpu.roll(jnp.where(end, prior, here), 1, 1)
            later = pltpu.roll(jnp.where(start, later, here), width - 1, 1)
            done.append((thick, tints, later - prior))
        for (part, at), (thick, tints, slope) in zip(places, done):
            thick_ref[z + part, at:at + group, :] = thick
            for k in range(3):
                tints_ref[k, z + part, at:at + group, :] = tints[k]
            slope_ref[z + part, at:at + group, :] = slope
        return carry

    lax.fori_loop(0, slices // deep, work, 0)


def first_matter_kernel(shift, total_z, active_ref, light_ref, gain_ref, bias_ref, field_ref, table_ref, *refs):
    make_table(total_z, active_ref, light_ref, gain_ref, bias_ref, table_ref)
    matter_kernel(shift, field_ref, table_ref, None, *refs)


def print_kernel(shift, part, views, field_ref, table_ref, left_ref, right_ref, after_ref, thick_ref, tints_ref, slope_ref,
                 *refs):
    blocks, slices, columns, width = field_ref.shape
    group = table_ref.shape[1]
    quad = columns // (2 * slices)
    count = columns // group
    block = lax.rem(lax.axis_index("depth") + shift, blocks - 1)
    slants = [[table_ref[9 + 4 * v + k] for k in range(3)] for v in range(views)]
    offsets = [table_ref[12 + 4 * v] for v in range(views)]
    line = lax.broadcasted_iota(jnp.int32, (group, width), 0)
    outs, sums = refs[:-4 * views], refs[-4 * views:]
    used = {"all": (0, 2 * columns), "own": (0, columns), "over": (columns, columns)}[part]
    for total in sums:
        total[pl.ds(*used), :] = jnp.zeros((used[1], width), jnp.float32)
    along = pl.ds(pl.multiple_of(block * width, width), width)
    tile = lax.axis_index("tile")
    left = left_ref[:, along].astype(jnp.float32) * jnp.where(tile > 0, 1.0, 0.0)
    right = right_ref[:, along].astype(jnp.float32) * jnp.where(tile + 1 < lax.axis_size("tile"), 1.0, 0.0)

    def wanted(v, j, z):
        first = j * group + z * (v + 1) * quad
        return first < columns if part == "own" else first + group > columns

    def work(j):
        base = j * group if isinstance(j, int) else pl.multiple_of(j * group, group)
        here_rows = pl.ds(base, group)
        for z in range(slices):
            chosen = [v for v in range(views) if part == "all" or wanted(v, j, z)]
            if not chosen:
                continue
            if isinstance(j, int) and j == 0:
                less = jnp.where(line == 0, left[z:z + 1, :], pltpu.roll(field_ref[block, z, here_rows, :], 1, 0))
            else:
                less = field_ref[block, z, pl.ds(base - 1, group), :]
            if isinstance(j, int) and j == count - 1:
                more = jnp.where(line == group - 1, right[z:z + 1, :],
                                 pltpu.roll(field_ref[block, z, here_rows, :], group - 1, 0))
            else:
                more = field_ref[block, z, pl.ds(base + 1, group), :]
            dx = more - less
            dy = slope_ref[z, here_rows, :]
            if z == 0:
                dz = field_ref[block, z + 1, here_rows, :]
            elif z == slices - 1:
                dz = -field_ref[block, z - 1, here_rows, :]
            else:
                dz = field_ref[block, z + 1, here_rows, :] - field_ref[block, z - 1, here_rows, :]
            steep = dx * dx + dy * dy + dz * dz
            thick = thick_ref[z, here_rows, :]
            tints = [tints_ref[k, z, here_rows, :] for k in range(3)]
            for v in chosen:
                place = pl.ds(base + z * (v + 1) * quad, group)
                lx, ly, lz = slants[v]
                facing = dx * lx + dy * ly + dz * lz
                shade = thick * ((-0.15 * LN2) - jnp.abs(facing) * lax.rsqrt(steep + offsets[v]))
                depth = sums[4 * v + 3][place, :]
                sums[4 * v + 3][place, :] = depth + thick
                shade = shade * lax.exp2(depth)
                for k in range(3):
                    sums[4 * v + k][place, :] = sums[4 * v + k][place, :] + tints[k] * shade

    if part == "all":
        work(count - 1)

        def inner(index, carry):
            work(count - 2 - index)
            return carry

        lax.fori_loop(0, count - 2, inner, 0)
        work(0)
    else:
        for j in range(count - 1, -1, -1):
            work(j)
    if part != "over":
        for v in range(views):
            for k in range(4):
                outs[0][v, k] = sums[4 * v + k][:columns, :]
    if part != "own":
        for v in range(views):
            first, size = over_rows(v, slices, columns)
            for k in range(4):
                rest = sums[4 * v + k][columns:columns + size, :]
                outs[-1][k, first:first + size, :] = encode(-rest if k == 3 else rest)


def over_rows(v, slices, columns):
    quad = columns // (2 * slices)
    ends = [-(-(slices - 1) * (view + 1) * quad // 16) * 16 for view in range(v + 1)]
    return sum(ends[:-1]), ends[-1]


def merged(own_ref, over_ref, v, slices):
    first, count = over_rows(v, slices, own_ref.shape[2])
    through = lax.exp2(own_ref[v, 3, :count, :])
    inside = jnp.where(lax.axis_index("tile") > 0, 1.0, 0.0)
    overs = [decode(over_ref[k, first:first + count, :]) * inside for k in range(4)]
    tops = [own_ref[v, k, :count, :] + through * overs[k] for k in range(3)] + [overs[3] - own_ref[v, 3, :count, :]]
    if count == own_ref.shape[2]:
        return tops
    lows = [own_ref[v, k, count:, :] * (1.0 if k < 3 else -1.0) for k in range(4)]
    return [jnp.concatenate([top, low]) for top, low in zip(tops, lows)]


def merge_kernel(slices, own_ref, over_ref, later_ref, arrived_ref, layer_ref, *passed_refs):
    for v in range(own_ref.shape[0]):
        for k, part in enumerate(merged(own_ref, over_ref, v, slices)):
            layer_ref[v, k] = encode(part)
    for ref in passed_refs:
        ref[...] = later_ref[...]


def final_kernel(views, share, slices, shifts, order_ref, own_ref, over_ref, *refs):
    layer_refs, image_ref = refs[:-1], refs[-1]
    groups = len(shifts) + 1
    owner = lax.axis_index("depth")
    ids = [owner] + [lax.rem(owner + groups - shift, groups) for shift in shifts]
    for v in range(views):
        order = [order_ref[v, r] for r in range(groups)]
        places = [sum(jnp.where(order[r] == one, r, 0) for r in range(groups)) for one in ids]
        layers = [merged(own_ref, over_ref, v, slices)] + [[ref[v, k] if ref.dtype == jnp.float32 else decode(ref[v, k]) for k in range(4)] for ref in layer_refs]
        colours = [0.0] * 3
        total = 0.0
        for g in range(groups):
            front = 0.0
            for h in range(groups):
                if h != g:
                    front = front + layers[h][3] * jnp.where(places[h] < places[g], 1.0, 0.0)
            through = lax.exp2(-front)
            colours = [colours[k] + layers[g][k] * through for k in range(3)]
            total = total + layers[g][3]
        for k, part in enumerate(colours + [1.0 - lax.exp2(-total)]):
            turned = part.T
            for t in range(turned.shape[0] // share):
                block = turned[t * share:(t + 1) * share, :]
                image_ref[t, v, k] = encode(block) if image_ref.dtype == jnp.int16 else block


def place_kernel(blocks_ref, image_ref):
    tiles, views, channels, share, columns = blocks_ref.shape
    for t in range(tiles):
        for v in range(views):
            for k in range(channels):
                block = blocks_ref[t, v, k]
                block = decode(block) if block.dtype == jnp.int16 else block
                image_ref[v, k, :, t * columns:(t + 1) * columns] = block


def turn_volume(volume, blocks):
    rows, slices, columns = volume.shape
    width = rows // blocks
    edge = jax.ShapeDtypeStruct((slices, rows), volume.dtype)
    return pl.pallas_call(
        turn_kernel,
        out_shape=[jax.ShapeDtypeStruct((blocks + 1, slices, columns, width), jnp.float32), edge, edge],
        in_specs=[vmem], out_specs=[vmem] * 3, scratch_shapes=[pltpu.VMEM((slices, rows, columns), volume.dtype)],
        cost_estimate=long_cost,
        compiler_params=turn_params, name="turn_rows")(volume)


def matter_of(field, shift, table=None, smalls=(), after=None):
    blocks, slices, columns, width = field.shape
    shape = (slices, columns, width)
    outs = [jax.ShapeDtypeStruct(shape, jnp.float32), jax.ShapeDtypeStruct((3,) + shape, jnp.float32),
            jax.ShapeDtypeStruct(shape, jnp.float32)]
    if table is not None:
        return pl.pallas_call(
            functools.partial(matter_kernel, shift), out_shape=outs, in_specs=[vmem] * 2 + [far], out_specs=[vmem] * 3,
            cost_estimate=short_cost, compiler_params=params, name="matter")(field, table, after)
    table = jax.ShapeDtypeStruct((9 + 4 * smalls[1].shape[0], 8, width), jnp.float32)
    return pl.pallas_call(
        functools.partial(first_matter_kernel, shift, slices * (blocks - 1)), out_shape=[table] + outs,
        in_specs=[vmem] + [smem] * 3 + [vmem], out_specs=[vmem] * 4,
        cost_estimate=short_cost, compiler_params=params, name="matter")(*smalls, field)


def prints_of(field, matter, table, left, right, after, shift, views, part):
    blocks, slices, columns, width = field.shape
    shape = (views, 4, columns, width)
    over_shape = (4, sum(over_rows(views - 1, slices, columns)), width)
    outs = [jax.ShapeDtypeStruct(shape, jnp.float32)] if part != "over" else []
    outs += [jax.ShapeDtypeStruct(over_shape, jnp.int16)] if part != "own" else []
    return pl.pallas_call(
        functools.partial(print_kernel, shift, part, views), out_shape=outs,
        in_specs=[vmem] * 4 + [far] + [vmem] * 3, out_specs=[vmem] * len(outs),
        scratch_shapes=[pltpu.VMEM((2 * columns, width), jnp.float32)] * (4 * views),
        cost_estimate=short_cost, compiler_params=params, name="prints")(field, table, left, right, after, *matter)


def merge_of(own, over, later, arrived, slices, passing):
    layer = jax.ShapeDtypeStruct(own.shape, jnp.int16)
    passed = [jax.ShapeDtypeStruct(later.shape, later.dtype)] if passing else []
    return pl.pallas_call(
        functools.partial(merge_kernel, slices), out_shape=[layer] + passed,
        in_specs=[vmem] * 2 + [vmem if passing else far, far], out_specs=[vmem] * (1 + len(passed)), cost_estimate=short_cost,
        compiler_params=params, name="merge")(own, over, later, arrived)


def open_kernel(layer_ref, opened_ref):
    for v in range(layer_ref.shape[0]):
        for k in range(layer_ref.shape[1]):
            opened_ref[v, k] = decode(layer_ref[v, k])


def open_of(layer):
    return pl.pallas_call(
        open_kernel, out_shape=jax.ShapeDtypeStruct(layer.shape, jnp.float32), in_specs=[vmem], out_specs=vmem,
        cost_estimate=long_cost, compiler_params=params, name="opened")(layer)


def final_of(depth_order, own, over, layers, shifts, share, slices):
    views, channels, columns, width = own.shape
    kind = jnp.int16 if share % 16 == 0 else jnp.float32
    return pl.pallas_call(
        functools.partial(final_kernel, views, share, slices, shifts),
        out_shape=jax.ShapeDtypeStruct((width // share, views, channels, share, columns), kind),
        in_specs=[smem] + [vmem] * (2 + len(layers)), out_specs=vmem, compiler_params=params,
        name="final")(depth_order, own, over, *layers)


def place_of(blocks):
    tiles, views, channels, share, columns = blocks.shape
    return pl.pallas_call(
        place_kernel, out_shape=jax.ShapeDtypeStruct((views, channels, share, tiles * columns), jnp.float32),
        in_specs=[vmem], out_specs=vmem, compiler_params=params, name="place")(blocks)


def passed_round(x, axis, by):
    devices = lax.axis_size(axis)
    return lax.ppermute(x, axis, [(i, (i + by) % devices) for i in range(devices)])


def local(volume, active, depth_order, light_vector, class_gain, class_bias):
    depth_count = lax.axis_size("depth")
    tile_count = lax.axis_size("tile")
    rows, slices, columns = volume.shape
    share = rows // (depth_count * tile_count)
    field, low, high = turn_volume(volume, depth_count)
    left = passed_round(high, "tile", 1)
    right = passed_round(low, "tile", -1)
    shifts = sorted(range(1, depth_count), key=lambda shift: -min(shift, depth_count - shift)) + [0]
    smalls = (active, light_vector, class_gain, class_bias)
    table, ready, waiting, layers = None, left, [], []
    views = light_vector.shape[0]
    for index, shift in enumerate(shifts):
        last = index + 1 == len(shifts)
        if index == 0:
            table, *matter = matter_of(field, shift, smalls=smalls)
            sources = field, matter, table, left, right
            over, = prints_of(*sources, ready, shift, views, "over")
            own, = prints_of(*sources, over, shift, views, "own")
        else:
            matter = matter_of(field, shift, table=table, after=ready)
            if len(waiting) > 1:
                ready, = merge_of(*waiting.pop(0), matter[0], ready, slices, False)
                layers.append(passed_round(ready, "depth", shifts[len(layers)]))
            own, over = prints_of(field, matter, table, left, right, ready, shift, views, "all")
        ready = own
        if index == 1 or last and waiting:
            ready, *passed = merge_of(*waiting.pop(0), over if last else own, ready, slices, last)
            over = passed[0] if last else over
            layers.append(passed_round(ready, "depth", shifts[len(layers)]))
        waiting.append((own, passed_round(over, "tile", 1)))
    layers = [open_of(layers[0])] + layers[1:]
    blocks = final_of(depth_order, *waiting[0], layers, shifts[:-1], share, slices)
    blocks = lax.all_to_all(blocks, "tile", split_axis=0, concat_axis=0, tiled=True)
    return place_of(blocks)


def solution(mesh):
    placed = (P(None, "depth", "tile"), P("depth", "tile"), P(), P(), P(), P())
    return jax.shard_map(
        local,
        mesh=mesh,
        in_specs=placed,
        out_specs=P(None, None, ("depth", "tile"), None),
        check_vma=False,
    )
```

```python
import functools
import math
import jax
import jax.numpy as jnp
from jax import lax
from jax.experimental import pallas as pl
from jax.experimental.pallas import tpu as pltpu
from jax.sharding import PartitionSpec as P

LN2 = math.log(2.0)
code_step = 1638.0
code_middle = 16.0
code_none = -32768.0

smem = pl.BlockSpec(memory_space=pltpu.SMEM)
vmem = pl.BlockSpec(memory_space=pltpu.VMEM)
far = pl.BlockSpec(memory_space=pl.ANY)
long_cost = pl.CostEstimate(flops=10**10, bytes_accessed=10**8, transcendentals=0)
short_cost = pl.CostEstimate(flops=10**8, bytes_accessed=10**6, transcendentals=0)
params = pltpu.CompilerParams(vmem_limit_bytes=12 * 1024 * 1024)
turn_params = pltpu.CompilerParams(vmem_limit_bytes=12 * 1024 * 1024)


def encode(x):
    return jnp.round(jnp.maximum(code_step * lax.log2(x) + code_step * code_middle, code_none)).astype(jnp.int16)


def decode(q):
    value = q.astype(jnp.int32).astype(jnp.float32)
    return jnp.where(value == code_none, 0.0, lax.exp2(value * (1.0 / code_step) - code_middle))


def turn_kernel(volume_ref, field_ref, low_ref, high_ref, ordered):
    rows, slices, columns = volume_ref.shape
    blocks, _, _, width = field_ref.shape
    blocks = blocks - 1

    def order(index, carry):
        at = pl.multiple_of(index * slices, slices)
        ordered[:, pl.ds(at, slices), :] = jnp.swapaxes(volume_ref[pl.ds(at, slices)], 0, 1)
        return carry

    lax.fori_loop(0, rows // slices, order, 0, unroll=4)
    field_ref[blocks] = jnp.zeros((slices, columns, width), jnp.float32)

    def turn(z, carry):
        for block in range(blocks):
            field_ref[block, z] = ordered[z, block * width:(block + 1) * width, :].T.astype(jnp.float32)
        return carry

    lax.fori_loop(0, slices, turn, 0)
    for edge_ref, x in ((low_ref, 0), (high_ref, columns - 1)):
        for block in range(blocks):
            edge_ref[:, block * width:(block + 1) * width] = field_ref[block, :, x, :].astype(edge_ref.dtype)


def make_table(total_z, active_ref, light_ref, gain_ref, bias_ref, table_ref):
    def spread(value):
        return jnp.full(table_ref.shape[1:], value, jnp.float32)

    values = [jnp.broadcast_to(active_ref[...].astype(jnp.float32) * (-2.0 / total_z), table_ref.shape[1:])]
    values += [spread(0.5 * gain_ref[k]) for k in range(3)] + [spread(gain_ref[3] * (1.0 / LN2))]
    values += [spread(0.5 * bias_ref[k]) for k in range(3)] + [spread(bias_ref[3] * (1.0 / LN2))]
    for v in range(light_ref.shape[0]):
        parts = [spread(light_ref[v, k]) for k in range(3)]
        square = jnp.maximum(parts[0] * parts[0] + parts[1] * parts[1] + parts[2] * parts[2], 1e-30)
        unit = (0.35 * LN2) * lax.rsqrt(square)
        values += [part * unit for part in parts] + [4.0 / square]
    for index, value in enumerate(values):
        table_ref[index] = value


def matter_kernel(shift, field_ref, table_ref, after_ref, thick_ref, tints_ref, slope_ref):
    slices, columns, width = thick_ref.shape
    group = table_ref.shape[1]
    scale = table_ref[0]
    gain = [table_ref[1 + k] for k in range(4)]
    bias = [table_ref[5 + k] for k in range(4)]
    lane = lax.broadcasted_iota(jnp.int32, (group, width), 1)
    start = lane == 0
    end = lane == width - 1
    deep = 2
    places = [(part, at * group) for part in range(deep) for at in range(columns // group)]
    blocks = field_ref.shape[0] - 1
    block = lax.rem(lax.axis_index("depth") + shift, blocks)
    before = jnp.where(block == 0, blocks, block - 1)
    behind = block + 1

    def work(step, carry):
        z = step * deep
        heres = [field_ref[block, z + part, at:at + group, :] for part, at in places]
        priors = [field_ref[before, z + part, at:at + group, :] for part, at in places]
        laters = [field_ref[behind, z + part, at:at + group, :] for part, at in places]
        done = []
        for here, prior, later in zip(heres, priors, laters):
            w = lax.exp2(gain[3] * here + bias[3])
            thick = scale * jnp.where(w < 0.001, w * (1.0 / LN2 - (0.5 / LN2) * w), lax.log2(1.0 + w))
            tints = [1.0 + jnp.tanh(gain[k] * here + bias[k]) for k in range(3)]
            prior = pltpu.roll(jnp.where(end, prior, here), 1, 1)
            later = pltpu.roll(jnp.where(start, later, here), width - 1, 1)
            done.append((thick, tints, later - prior))
        for (part, at), (thick, tints, slope) in zip(places, done):
            thick_ref[z + part, at:at + group, :] = thick
            for k in range(3):
                tints_ref[k, z + part, at:at + group, :] = tints[k]
            slope_ref[z + part, at:at + group, :] = slope
        return carry

    lax.fori_loop(0, slices // deep, work, 0)


def first_matter_kernel(shift, total_z, active_ref, light_ref, gain_ref, bias_ref, field_ref, table_ref, *refs):
    make_table(total_z, active_ref, light_ref, gain_ref, bias_ref, table_ref)
    matter_kernel(shift, field_ref, table_ref, None, *refs)


def print_kernel(shift, part, views, field_ref, table_ref, left_ref, right_ref, after_ref, thick_ref, tints_ref, slope_ref,
                 *refs):
    blocks, slices, columns, width = field_ref.shape
    group = table_ref.shape[1]
    quad = columns // (2 * slices)
    count = columns // group
    block = lax.rem(lax.axis_index("depth") + shift, blocks - 1)
    slants = [[table_ref[9 + 4 * v + k] for k in range(3)] for v in range(views)]
    offsets = [table_ref[12 + 4 * v] for v in range(views)]
    line = lax.broadcasted_iota(jnp.int32, (group, width), 0)
    outs, sums = refs[:-4 * views], refs[-4 * views:]
    used = {"all": (0, 2 * columns), "own": (0, columns + group), "over": (columns - group, columns + group)}[part]
    for total in sums:
        total[pl.ds(*used), :] = jnp.zeros((used[1], width), jnp.float32)
    along = pl.ds(pl.multiple_of(block * width, width), width)
    tile = lax.axis_index("tile")
    left = left_ref[:, along].astype(jnp.float32) * jnp.where(tile > 0, 1.0, 0.0)
    right = right_ref[:, along].astype(jnp.float32) * jnp.where(tile + 1 < lax.axis_size("tile"), 1.0, 0.0)

    def wanted(v, j, z):
        first = j * group + z * (v + 1) * quad
        return first < columns if part == "own" else first + group > columns

    def work(j):
        base = j * group if isinstance(j, int) else pl.multiple_of(j * group, group)
        here_rows = pl.ds(base, group)
        for z in range(slices):
            chosen = [v for v in range(views) if part == "all" or wanted(v, j, z)]
            if not chosen:
                continue
            if isinstance(j, int) and j == 0:
                less = jnp.where(line == 0, left[z:z + 1, :], pltpu.roll(field_ref[block, z, here_rows, :], 1, 0))
            else:
                less = field_ref[block, z, pl.ds(base - 1, group), :]
            if isinstance(j, int) and j == count - 1:
                more = jnp.where(line == group - 1, right[z:z + 1, :],
                                 pltpu.roll(field_ref[block, z, here_rows, :], group - 1, 0))
            else:
                more = field_ref[block, z, pl.ds(base + 1, group), :]
            dx = more - less
            dy = slope_ref[z, here_rows, :]
            if z == 0:
                dz = field_ref[block, z + 1, here_rows, :]
            elif z == slices - 1:
                dz = -field_ref[block, z - 1, here_rows, :]
            else:
                dz = field_ref[block, z + 1, here_rows, :] - field_ref[block, z - 1, here_rows, :]
            steep = dx * dx + dy * dy + dz * dz
            thick = thick_ref[z, here_rows, :]
            tints = [tints_ref[k, z, here_rows, :] for k in range(3)]
            for v in chosen:
                place = pl.ds(base + z * (v + 1) * quad, group)
                lx, ly, lz = slants[v]
                facing = dx * lx + dy * ly + dz * lz
                shade = thick * ((-0.15 * LN2) - jnp.abs(facing) * lax.rsqrt(steep + offsets[v]))
                depth = sums[4 * v + 3][place, :]
                sums[4 * v + 3][place, :] = depth + thick
                shade = shade * lax.exp2(depth)
                for k in range(3):
                    sums[4 * v + k][place, :] = sums[4 * v + k][place, :] + tints[k] * shade

    if part == "all":
        work(count - 1)

        def inner(index, carry):
            work(count - 2 - index)
            return carry

        lax.fori_loop(0, count - 2, inner, 0)
        work(0)
    else:
        for j in range(count - 1, -1, -1):
            work(j)
    if part != "over":
        for v in range(views):
            for k in range(4):
                outs[0][v, k] = sums[4 * v + k][:columns, :]
    if part != "own":
        for v in range(views):
            first, size = over_rows(v, slices, columns)
            for k in range(4):
                rest = sums[4 * v + k][columns:columns + size, :]
                outs[-1][k, first:first + size, :] = encode(-rest if k == 3 else rest)


def over_rows(v, slices, columns):
    quad = columns // (2 * slices)
    ends = [-(-(slices - 1) * (view + 1) * quad // 16) * 16 for view in range(v + 1)]
    return sum(ends[:-1]), ends[-1]


def merged(own_ref, over_ref, v, slices):
    first, count = over_rows(v, slices, own_ref.shape[2])
    through = lax.exp2(own_ref[v, 3, :count, :])
    inside = jnp.where(lax.axis_index("tile") > 0, 1.0, 0.0)
    overs = [decode(over_ref[k, first:first + count, :]) * inside for k in range(4)]
    tops = [own_ref[v, k, :count, :] + through * overs[k] for k in range(3)] + [overs[3] - own_ref[v, 3, :count, :]]
    if count == own_ref.shape[2]:
        return tops
    lows = [own_ref[v, k, count:, :] * (1.0 if k < 3 else -1.0) for k in range(4)]
    return [jnp.concatenate([top, low]) for top, low in zip(tops, lows)]


def merge_kernel(slices, own_ref, over_ref, later_ref, arrived_ref, layer_ref, *passed_refs):
    for v in range(own_ref.shape[0]):
        for k, part in enumerate(merged(own_ref, over_ref, v, slices)):
            layer_ref[v, k] = encode(part)
    for ref in passed_refs:
        ref[...] = later_ref[...]


def early_kernel(slices, shifts, order_ref, own_ref, over_ref, *refs):
    layer_refs, mix_ref = refs[:-1], refs[-1]
    groups = len(shifts) + 1
    owner = lax.axis_index("depth")
    ids = [owner] + [lax.rem(owner + groups - shift, groups) for shift in shifts]
    for v in range(own_ref.shape[0]):
        order = [order_ref[v, r] for r in range(groups)]
        places = [sum(jnp.where(order[r] == one, r, 0) for r in range(groups)) for one in ids]
        layers = [merged(own_ref, over_ref, v, slices)]
        layers += [[ref[v, k] if ref.dtype == jnp.float32 else decode(ref[v, k]) for k in range(4)] for ref in layer_refs]
        ahead = [0.0] * 3
        after = [0.0] * 3
        depth_ahead = 0.0
        total = 0.0
        for g in range(groups - 1):
            front = 0.0
            for h in range(groups - 1):
                if h != g:
                    front = front + layers[h][3] * jnp.where(places[h] < places[g], 1.0, 0.0)
            first = jnp.where(places[g] < places[-1], 1.0, 0.0)
            through = lax.exp2(-front)
            near, far_off = through * first, through * (1.0 - first)
            ahead = [ahead[k] + layers[g][k] * near for k in range(3)]
            after = [after[k] + layers[g][k] * far_off for k in range(3)]
            depth_ahead = depth_ahead + layers[g][3] * first
            total = total + layers[g][3]
        for k, part in enumerate(ahead + after + [lax.exp2(-depth_ahead), total]):
            mix_ref[v, k] = part


def final_kernel(share, mix_ref, layer_ref, image_ref):
    for v in range(mix_ref.shape[0]):
        depth = decode(layer_ref[v, 3])
        through = lax.exp2(-depth)
        colours = [mix_ref[v, k] + mix_ref[v, 6] * decode(layer_ref[v, k]) + through * mix_ref[v, 3 + k] for k in range(3)]
        for k, part in enumerate(colours + [1.0 - lax.exp2(-(mix_ref[v, 7] + depth))]):
            turned = part.T
            for t in range(turned.shape[0] // share):
                block = turned[t * share:(t + 1) * share, :]
                image_ref[t, v, k] = encode(block) if image_ref.dtype == jnp.int16 else block


def place_kernel(blocks_ref, image_ref):
    tiles, views, channels, share, columns = blocks_ref.shape
    for t in range(tiles):
        for v in range(views):
            for k in range(channels):
                block = blocks_ref[t, v, k]
                block = decode(block) if block.dtype == jnp.int16 else block
                image_ref[v, k, :, t * columns:(t + 1) * columns] = block


def turn_volume(volume, blocks):
    rows, slices, columns = volume.shape
    width = rows // blocks
    edge = jax.ShapeDtypeStruct((slices, rows), volume.dtype)
    return pl.pallas_call(
        turn_kernel,
        out_shape=[jax.ShapeDtypeStruct((blocks + 1, slices, columns, width), jnp.float32), edge, edge],
        in_specs=[vmem], out_specs=[vmem] * 3, scratch_shapes=[pltpu.VMEM((slices, rows, columns), volume.dtype)],
        cost_estimate=long_cost,
        compiler_params=turn_params, name="turn_rows")(volume)


def matter_of(field, shift, table=None, smalls=(), after=None):
    blocks, slices, columns, width = field.shape
    shape = (slices, columns, width)
    outs = [jax.ShapeDtypeStruct(shape, jnp.float32), jax.ShapeDtypeStruct((3,) + shape, jnp.float32),
            jax.ShapeDtypeStruct(shape, jnp.float32)]
    if table is not None:
        return pl.pallas_call(
            functools.partial(matter_kernel, shift), out_shape=outs, in_specs=[vmem] * 2 + [far], out_specs=[vmem] * 3,
            cost_estimate=short_cost, compiler_params=params, name="matter")(field, table, after)
    table = jax.ShapeDtypeStruct((9 + 4 * smalls[1].shape[0], 8, width), jnp.float32)
    return pl.pallas_call(
        functools.partial(first_matter_kernel, shift, slices * (blocks - 1)), out_shape=[table] + outs,
        in_specs=[vmem] + [smem] * 3 + [vmem], out_specs=[vmem] * 4,
        cost_estimate=short_cost, compiler_params=params, name="matter")(*smalls, field)


def prints_of(field, matter, table, left, right, after, shift, views, part):
    blocks, slices, columns, width = field.shape
    shape = (views, 4, columns, width)
    over_shape = (4, sum(over_rows(views - 1, slices, columns)), width)
    outs = [jax.ShapeDtypeStruct(shape, jnp.float32)] if part != "over" else []
    outs += [jax.ShapeDtypeStruct(over_shape, jnp.int16)] if part != "own" else []
    return pl.pallas_call(
        functools.partial(print_kernel, shift, part, views), out_shape=outs,
        in_specs=[vmem] * 4 + [far] + [vmem] * 3, out_specs=[vmem] * len(outs),
        scratch_shapes=[pltpu.VMEM((2 * columns, width), jnp.float32)] * (4 * views),
        cost_estimate=short_cost, compiler_params=params, name="prints")(field, table, left, right, after, *matter)


def merge_of(own, over, later, arrived, slices, passing):
    layer = jax.ShapeDtypeStruct(own.shape, jnp.int16)
    passed = [jax.ShapeDtypeStruct(later.shape, later.dtype)] if passing else []
    return pl.pallas_call(
        functools.partial(merge_kernel, slices), out_shape=[layer] + passed,
        in_specs=[vmem] * 2 + [vmem if passing else far, far], out_specs=[vmem] * (1 + len(passed)), cost_estimate=short_cost,
        compiler_params=params, name="merge")(own, over, later, arrived)


def open_kernel(layer_ref, opened_ref):
    for v in range(layer_ref.shape[0]):
        for k in range(layer_ref.shape[1]):
            opened_ref[v, k] = decode(layer_ref[v, k])


def open_of(layer):
    return pl.pallas_call(
        open_kernel, out_shape=jax.ShapeDtypeStruct(layer.shape, jnp.float32), in_specs=[vmem], out_specs=vmem,
        cost_estimate=long_cost, compiler_params=params, name="opened")(layer)


def early_of(depth_order, own, over, layers, shifts, slices):
    views, channels, columns, width = own.shape
    return pl.pallas_call(
        functools.partial(early_kernel, slices, shifts), out_shape=jax.ShapeDtypeStruct((views, 8, columns, width), jnp.float32),
        in_specs=[smem] + [vmem] * (2 + len(layers)), out_specs=vmem, cost_estimate=short_cost,
        compiler_params=params, name="early")(depth_order, own, over, *layers)


def final_of(mix, layer, share):
    views, channels, columns, width = layer.shape
    kind = jnp.int16 if share % 16 == 0 else jnp.float32
    return pl.pallas_call(
        functools.partial(final_kernel, share),
        out_shape=jax.ShapeDtypeStruct((width // share, views, channels, share, columns), kind),
        in_specs=[vmem] * 2, out_specs=vmem, compiler_params=params, name="final")(mix, layer)


def place_of(blocks):
    tiles, views, channels, share, columns = blocks.shape
    return pl.pallas_call(
        place_kernel, out_shape=jax.ShapeDtypeStruct((views, channels, share, tiles * columns), jnp.float32),
        in_specs=[vmem], out_specs=vmem, compiler_params=params, name="place")(blocks)


def passed_round(x, axis, by):
    devices = lax.axis_size(axis)
    return lax.ppermute(x, axis, [(i, (i + by) % devices) for i in range(devices)])


def local(volume, active, depth_order, light_vector, class_gain, class_bias):
    depth_count = lax.axis_size("depth")
    tile_count = lax.axis_size("tile")
    rows, slices, columns = volume.shape
    share = rows // (depth_count * tile_count)
    field, low, high = turn_volume(volume, depth_count)
    left = passed_round(high, "tile", 1)
    right = passed_round(low, "tile", -1)
    shifts = sorted(range(1, depth_count), key=lambda shift: -min(shift, depth_count - shift)) + [0]
    smalls = (active, light_vector, class_gain, class_bias)
    table, ready, waiting, layers = None, left, [], []
    views = light_vector.shape[0]
    for index, shift in enumerate(shifts):
        last = index + 1 == len(shifts)
        if index == 0:
            table, *matter = matter_of(field, shift, smalls=smalls)
            sources = field, matter, table, left, right
            over, = prints_of(*sources, ready, shift, views, "over")
            own, = prints_of(*sources, over, shift, views, "own")
        else:
            matter = matter_of(field, shift, table=table, after=ready)
            if len(waiting) > 1:
                ready, = merge_of(*waiting.pop(0), matter[0], ready, slices, False)
                layers.append(passed_round(ready, "depth", shifts[len(layers)]))
            own, over = prints_of(field, matter, table, left, right, ready, shift, views, "all")
        ready = own
        if index == 1 or last and waiting:
            ready, *passed = merge_of(*waiting.pop(0), over if last else own, ready, slices, last)
            over = passed[0] if last else over
            layers.append(passed_round(ready, "depth", shifts[len(layers)]))
        waiting.append((own, passed_round(over, "tile", 1)))
    mix = early_of(depth_order, *waiting[0], [open_of(layers[0])] + layers[1:-1], shifts[:-1], slices)
    blocks = final_of(mix, layers[-1], share)
    blocks = lax.all_to_all(blocks, "tile", split_axis=0, concat_axis=0, tiled=True)
    return place_of(blocks)


def solution(mesh):
    placed = (P(None, "depth", "tile"), P("depth", "tile"), P(), P(), P(), P())
    return jax.shard_map(
        local,
        mesh=mesh,
        in_specs=placed,
        out_specs=P(None, None, ("depth", "tile"), None),
        check_vma=False,
    )
```

```python
import functools
import math
import jax
import jax.numpy as jnp
from jax import lax
from jax.experimental import pallas as pl
from jax.experimental.pallas import tpu as pltpu
from jax.sharding import PartitionSpec as P

LN2 = math.log(2.0)
code_step = 1638.0
code_middle = 16.0
code_none = -32768.0

smem = pl.BlockSpec(memory_space=pltpu.SMEM)
vmem = pl.BlockSpec(memory_space=pltpu.VMEM)
far = pl.BlockSpec(memory_space=pl.ANY)
long_cost = pl.CostEstimate(flops=10**10, bytes_accessed=10**8, transcendentals=0)
short_cost = pl.CostEstimate(flops=10**8, bytes_accessed=10**6, transcendentals=0)
params = pltpu.CompilerParams(vmem_limit_bytes=12 * 1024 * 1024)
turn_params = pltpu.CompilerParams(vmem_limit_bytes=12 * 1024 * 1024)


def encode(x):
    return jnp.round(jnp.maximum(code_step * lax.log2(x) + code_step * code_middle, code_none)).astype(jnp.int16)


def decode(q):
    value = q.astype(jnp.int32).astype(jnp.float32)
    return jnp.where(value == code_none, 0.0, lax.exp2(value * (1.0 / code_step) - code_middle))


def turn_kernel(volume_ref, field_ref, near_ref, far_ref, ordered):
    rows, slices, columns = volume_ref.shape
    blocks, _, _, width = field_ref.shape
    blocks = blocks - 1

    def order(index, carry):
        at = pl.multiple_of(index * slices, slices)
        ordered[:, pl.ds(at, slices), :] = jnp.swapaxes(volume_ref[pl.ds(at, slices)], 0, 1)
        return carry

    lax.fori_loop(0, rows // slices, order, 0, unroll=4)
    field_ref[blocks] = jnp.zeros((slices, columns, width), jnp.float32)

    def turn(z, carry):
        for block in range(blocks):
            field_ref[block, z] = ordered[z, block * width:(block + 1) * width, :].T.astype(jnp.float32)
        return carry

    lax.fori_loop(0, slices, turn, 0)
    even = lax.rem(lax.axis_index("tile"), 2) == 0
    for block in range(blocks):
        low, high = field_ref[block, :, 0, :], field_ref[block, :, columns - 1, :]
        along = slice(block * width, (block + 1) * width)
        near_ref[:, along] = jnp.where(even, high, low).astype(near_ref.dtype)
        far_ref[:, along] = jnp.where(even, low, high).astype(far_ref.dtype)


def make_table(total_z, active_ref, light_ref, gain_ref, bias_ref, table_ref):
    def wide(ref, k):
        return jnp.broadcast_to(ref[:, k:k + 1], table_ref.shape[1:])

    values = [jnp.broadcast_to(active_ref[...].astype(jnp.float32) * (-2.0 / total_z), table_ref.shape[1:])]
    values += [0.5 * wide(gain_ref, k) for k in range(3)] + [wide(gain_ref, 3) * (1.0 / LN2)]
    values += [0.5 * wide(bias_ref, k) for k in range(3)] + [wide(bias_ref, 3) * (1.0 / LN2)]
    for v in range(light_ref.shape[0]):
        parts = [jnp.broadcast_to(light_ref[v:v + 1, k:k + 1], table_ref.shape[1:]) for k in range(3)]
        square = jnp.maximum(parts[0] * parts[0] + parts[1] * parts[1] + parts[2] * parts[2], 1e-30)
        unit = (0.35 * LN2) * lax.rsqrt(square)
        values += [part * unit for part in parts] + [4.0 / square]
    for index, value in enumerate(values):
        table_ref[index] = value


def matter_kernel(shift, field_ref, table_ref, after_ref, thick_ref, tints_ref, slope_ref):
    slices, columns, width = thick_ref.shape
    group = table_ref.shape[1]
    scale = table_ref[0]
    gain = [table_ref[1 + k] for k in range(4)]
    bias = [table_ref[5 + k] for k in range(4)]
    lane = lax.broadcasted_iota(jnp.int32, (group, width), 1)
    start = lane == 0
    end = lane == width - 1
    deep = 2
    places = [(part, at * group) for part in range(deep) for at in range(columns // group)]
    blocks = field_ref.shape[0] - 1
    block = lax.rem(lax.axis_index("depth") + shift, blocks)
    before = jnp.where(block == 0, blocks, block - 1)
    behind = block + 1

    def work(step, carry):
        z = step * deep
        heres = [field_ref[block, z + part, at:at + group, :] for part, at in places]
        priors = [field_ref[before, z + part, at:at + group, :] for part, at in places]
        laters = [field_ref[behind, z + part, at:at + group, :] for part, at in places]
        done = []
        for here, prior, later in zip(heres, priors, laters):
            w = lax.exp2(gain[3] * here + bias[3])
            thick = scale * jnp.where(w < 0.001, w * (1.0 / LN2 - (0.5 / LN2) * w), lax.log2(1.0 + w))
            tints = [1.0 + jnp.tanh(gain[k] * here + bias[k]) for k in range(3)]
            prior = pltpu.roll(jnp.where(end, prior, here), 1, 1)
            later = pltpu.roll(jnp.where(start, later, here), width - 1, 1)
            done.append((thick, tints, later - prior))
        for (part, at), (thick, tints, slope) in zip(places, done):
            thick_ref[z + part, at:at + group, :] = thick
            for k in range(3):
                tints_ref[k, z + part, at:at + group, :] = tints[k]
            slope_ref[z + part, at:at + group, :] = slope
        return carry

    lax.fori_loop(0, slices // deep, work, 0)


def first_matter_kernel(shift, total_z, active_ref, light_ref, gain_ref, bias_ref, field_ref, table_ref, *refs):
    make_table(total_z, active_ref, light_ref, gain_ref, bias_ref, table_ref)
    matter_kernel(shift, field_ref, table_ref, None, *refs)


def print_kernel(shift, part, views, field_ref, table_ref, near_ref, far_ref, after_ref, thick_ref, tints_ref, slope_ref,
                 *refs):
    blocks, slices, columns, width = field_ref.shape
    group = table_ref.shape[1]
    quad = columns // (2 * slices)
    count = columns // group
    block = lax.rem(lax.axis_index("depth") + shift, blocks - 1)
    slants = [[table_ref[9 + 4 * v + k] for k in range(3)] for v in range(views)]
    offsets = [table_ref[12 + 4 * v] for v in range(views)]
    line = lax.broadcasted_iota(jnp.int32, (group, width), 0)
    outs, sums = refs[:-4 * views], refs[-4 * views:]
    used = {"all": (0, 2 * columns), "own": (0, columns + group), "over": (columns - group, columns + group)}[part]
    for total in sums:
        total[pl.ds(*used), :] = jnp.zeros((used[1], width), jnp.float32)
    along = pl.ds(pl.multiple_of(block * width, width), width)
    tile = lax.axis_index("tile")
    even = lax.rem(tile, 2) == 0
    near = near_ref[:, along].astype(jnp.float32)
    far_edge = far_ref[:, along].astype(jnp.float32)
    left = jnp.where(even, far_edge, near) * jnp.where(tile > 0, 1.0, 0.0)
    right = jnp.where(even, near, far_edge) * jnp.where(tile + 1 < lax.axis_size("tile"), 1.0, 0.0)

    def wanted(v, j, z):
        first = j * group + z * (v + 1) * quad
        return first < columns if part == "own" else first + group > columns

    def work(j):
        base = j * group if isinstance(j, int) else pl.multiple_of(j * group, group)
        here_rows = pl.ds(base, group)
        for z in range(slices):
            chosen = [v for v in range(views) if part == "all" or wanted(v, j, z)]
            if not chosen:
                continue
            if isinstance(j, int) and j == 0:
                less = jnp.where(line == 0, left[z:z + 1, :], pltpu.roll(field_ref[block, z, here_rows, :], 1, 0))
            else:
                less = field_ref[block, z, pl.ds(base - 1, group), :]
            if isinstance(j, int) and j == count - 1:
                more = jnp.where(line == group - 1, right[z:z + 1, :],
                                 pltpu.roll(field_ref[block, z, here_rows, :], group - 1, 0))
            else:
                more = field_ref[block, z, pl.ds(base + 1, group), :]
            dx = more - less
            dy = slope_ref[z, here_rows, :]
            if z == 0:
                dz = field_ref[block, z + 1, here_rows, :]
            elif z == slices - 1:
                dz = -field_ref[block, z - 1, here_rows, :]
            else:
                dz = field_ref[block, z + 1, here_rows, :] - field_ref[block, z - 1, here_rows, :]
            steep = dx * dx + dy * dy + dz * dz
            thick = thick_ref[z, here_rows, :]
            tints = [tints_ref[k, z, here_rows, :] for k in range(3)]
            for v in chosen:
                place = pl.ds(base + z * (v + 1) * quad, group)
                lx, ly, lz = slants[v]
                facing = dx * lx + dy * ly + dz * lz
                shade = thick * ((-0.15 * LN2) - jnp.abs(facing) * lax.rsqrt(steep + offsets[v]))
                depth = sums[4 * v + 3][place, :]
                sums[4 * v + 3][place, :] = depth + thick
                shade = shade * lax.exp2(depth)
                for k in range(3):
                    sums[4 * v + k][place, :] = sums[4 * v + k][place, :] + tints[k] * shade

    if part == "all":
        work(count - 1)

        def inner(index, carry):
            work(count - 2 - index)
            return carry

        lax.fori_loop(0, count - 2, inner, 0)
        work(0)
    else:
        for j in range(count - 1, -1, -1):
            work(j)
    if part != "over":
        for v in range(views):
            for k in range(4):
                outs[0][v, k] = sums[4 * v + k][:columns, :]
    if part != "own":
        for v in range(views):
            first, size = over_rows(v, slices, columns)
            for k in range(4):
                rest = sums[4 * v + k][columns:columns + size, :]
                outs[-1][k, first:first + size, :] = encode(-rest if k == 3 else rest)


def over_rows(v, slices, columns):
    quad = columns // (2 * slices)
    ends = [-(-(slices - 1) * (view + 1) * quad // 16) * 16 for view in range(v + 1)]
    return sum(ends[:-1]), ends[-1]


def merged(own_ref, over_ref, v, slices):
    first, count = over_rows(v, slices, own_ref.shape[2])
    through = lax.exp2(own_ref[v, 3, :count, :])
    inside = jnp.where(lax.axis_index("tile") > 0, 1.0, 0.0)
    overs = [decode(over_ref[k, first:first + count, :]) * inside for k in range(4)]
    tops = [own_ref[v, k, :count, :] + through * overs[k] for k in range(3)] + [overs[3] - own_ref[v, 3, :count, :]]
    if count == own_ref.shape[2]:
        return tops
    lows = [own_ref[v, k, count:, :] * (1.0 if k < 3 else -1.0) for k in range(4)]
    return [jnp.concatenate([top, low]) for top, low in zip(tops, lows)]


def merge_kernel(slices, own_ref, over_ref, later_ref, arrived_ref, layer_ref, *passed_refs):
    for v in range(own_ref.shape[0]):
        for k, part in enumerate(merged(own_ref, over_ref, v, slices)):
            layer_ref[v, k] = encode(part)
    for ref in passed_refs:
        ref[...] = later_ref[...]


def early_kernel(slices, shifts, order_ref, own_ref, over_ref, *refs):
    layer_refs, mix_ref = refs[:-1], refs[-1]
    groups = len(shifts) + 1
    owner = lax.axis_index("depth")
    ids = [owner] + [lax.rem(owner + groups - shift, groups) for shift in shifts]
    for v in range(own_ref.shape[0]):
        order = [order_ref[v, r] for r in range(groups)]
        places = [sum(jnp.where(order[r] == one, r, 0) for r in range(groups)) for one in ids]
        layers = [merged(own_ref, over_ref, v, slices)]
        layers += [[ref[v, k] if ref.dtype == jnp.float32 else decode(ref[v, k]) for k in range(4)] for ref in layer_refs]
        ahead = [0.0] * 3
        after = [0.0] * 3
        depth_ahead = 0.0
        total = 0.0
        for g in range(groups - 1):
            front = 0.0
            for h in range(groups - 1):
                if h != g:
                    front = front + layers[h][3] * jnp.where(places[h] < places[g], 1.0, 0.0)
            first = jnp.where(places[g] < places[-1], 1.0, 0.0)
            through = lax.exp2(-front)
            near, far_off = through * first, through * (1.0 - first)
            ahead = [ahead[k] + layers[g][k] * near for k in range(3)]
            after = [after[k] + layers[g][k] * far_off for k in range(3)]
            depth_ahead = depth_ahead + layers[g][3] * first
            total = total + layers[g][3]
        for k, part in enumerate(ahead + after + [lax.exp2(-depth_ahead), total]):
            mix_ref[v, k] = part


def final_kernel(share, mix_ref, layer_ref, image_ref):
    for v in range(mix_ref.shape[0]):
        depth = decode(layer_ref[v, 3])
        through = lax.exp2(-depth)
        colours = [mix_ref[v, k] + mix_ref[v, 6] * decode(layer_ref[v, k]) + through * mix_ref[v, 3 + k] for k in range(3)]
        for k, part in enumerate(colours + [1.0 - lax.exp2(-(mix_ref[v, 7] + depth))]):
            turned = part.T
            for t in range(turned.shape[0] // share):
                block = turned[t * share:(t + 1) * share, :]
                image_ref[t, v, k] = encode(block) if image_ref.dtype == jnp.int16 else block


def place_kernel(blocks_ref, image_ref):
    tiles, views, channels, share, columns = blocks_ref.shape
    for t in range(tiles):
        for v in range(views):
            for k in range(channels):
                block = blocks_ref[t, v, k]
                block = decode(block) if block.dtype == jnp.int16 else block
                image_ref[v, k, :, t * columns:(t + 1) * columns] = block


def turn_volume(volume, blocks):
    rows, slices, columns = volume.shape
    width = rows // blocks
    edge = jax.ShapeDtypeStruct((slices, rows), volume.dtype)
    return pl.pallas_call(
        turn_kernel,
        out_shape=[jax.ShapeDtypeStruct((blocks + 1, slices, columns, width), jnp.float32), edge, edge],
        in_specs=[vmem], out_specs=[vmem] * 3, scratch_shapes=[pltpu.VMEM((slices, rows, columns), volume.dtype)],
        cost_estimate=long_cost,
        compiler_params=turn_params, name="turn_rows")(volume)


def matter_of(field, shift, table=None, smalls=(), after=None):
    blocks, slices, columns, width = field.shape
    shape = (slices, columns, width)
    outs = [jax.ShapeDtypeStruct(shape, jnp.float32), jax.ShapeDtypeStruct((3,) + shape, jnp.float32),
            jax.ShapeDtypeStruct(shape, jnp.float32)]
    if table is not None:
        return pl.pallas_call(
            functools.partial(matter_kernel, shift), out_shape=outs, in_specs=[vmem] * 2 + [far], out_specs=[vmem] * 3,
            cost_estimate=short_cost, compiler_params=params, name="matter")(field, table, after)
    table = jax.ShapeDtypeStruct((9 + 4 * smalls[1].shape[0], 8, width), jnp.float32)
    return pl.pallas_call(
        functools.partial(first_matter_kernel, shift, slices * (blocks - 1)), out_shape=[table] + outs,
        in_specs=[vmem] * 5, out_specs=[vmem] * 4,
        cost_estimate=short_cost, compiler_params=params, name="matter")(*smalls, field)


def prints_of(field, matter, table, near, beyond, after, shift, views, part):
    blocks, slices, columns, width = field.shape
    shape = (views, 4, columns, width)
    over_shape = (4, sum(over_rows(views - 1, slices, columns)), width)
    outs = [jax.ShapeDtypeStruct(shape, jnp.float32)] if part != "over" else []
    outs += [jax.ShapeDtypeStruct(over_shape, jnp.int16)] if part != "own" else []
    return pl.pallas_call(
        functools.partial(print_kernel, shift, part, views), out_shape=outs,
        in_specs=[vmem] * 4 + [far] + [vmem] * 3, out_specs=[vmem] * len(outs),
        scratch_shapes=[pltpu.VMEM((2 * columns, width), jnp.float32)] * (4 * views),
        cost_estimate=short_cost, compiler_params=params, name="prints")(field, table, near, beyond, after, *matter)


def merge_of(own, over, later, arrived, slices, passing):
    layer = jax.ShapeDtypeStruct(own.shape, jnp.int16)
    passed = [jax.ShapeDtypeStruct(later.shape, later.dtype)] if passing else []
    return pl.pallas_call(
        functools.partial(merge_kernel, slices), out_shape=[layer] + passed,
        in_specs=[vmem] * 2 + [vmem if passing else far, far], out_specs=[vmem] * (1 + len(passed)), cost_estimate=short_cost,
        compiler_params=params, name="merge")(own, over, later, arrived)


def open_kernel(layer_ref, opened_ref):
    for v in range(layer_ref.shape[0]):
        for k in range(layer_ref.shape[1]):
            opened_ref[v, k] = decode(layer_ref[v, k])


def open_of(layer):
    return pl.pallas_call(
        open_kernel, out_shape=jax.ShapeDtypeStruct(layer.shape, jnp.float32), in_specs=[vmem], out_specs=vmem,
        cost_estimate=long_cost, compiler_params=params, name="opened")(layer)


def early_of(depth_order, own, over, layers, shifts, slices):
    views, channels, columns, width = own.shape
    return pl.pallas_call(
        functools.partial(early_kernel, slices, shifts), out_shape=jax.ShapeDtypeStruct((views, 8, columns, width), jnp.float32),
        in_specs=[smem] + [vmem] * (2 + len(layers)), out_specs=vmem, cost_estimate=short_cost,
        compiler_params=params, name="early")(depth_order, own, over, *layers)


def final_of(mix, layer, share):
    views, channels, columns, width = layer.shape
    kind = jnp.int16 if share % 16 == 0 else jnp.float32
    return pl.pallas_call(
        functools.partial(final_kernel, share),
        out_shape=jax.ShapeDtypeStruct((width // share, views, channels, share, columns), kind),
        in_specs=[vmem] * 2, out_specs=vmem, compiler_params=params, name="final")(mix, layer)


def place_of(blocks):
    tiles, views, channels, share, columns = blocks.shape
    return pl.pallas_call(
        place_kernel, out_shape=jax.ShapeDtypeStruct((views, channels, share, tiles * columns), jnp.float32),
        in_specs=[vmem], out_specs=vmem, compiler_params=params, name="place")(blocks)


def passed_round(x, axis, by):
    devices = lax.axis_size(axis)
    return lax.ppermute(x, axis, [(i, (i + by) % devices) for i in range(devices)])


def swapped(x, axis, by):
    devices = lax.axis_size(axis)
    pairs = [(i, (i + by * (1 - 2 * (i % 2))) % devices) for i in range(devices)]
    return lax.ppermute(x, axis, pairs)


def local(volume, active, depth_order, light_vector, class_gain, class_bias):
    depth_count = lax.axis_size("depth")
    tile_count = lax.axis_size("tile")
    rows, slices, columns = volume.shape
    share = rows // (depth_count * tile_count)
    field, to_near, to_beyond = turn_volume(volume, depth_count)
    beyond = swapped(to_beyond, "tile", -1)
    near = swapped(to_near, "tile", 1)
    shifts = sorted(range(1, depth_count), key=lambda shift: -min(shift, depth_count - shift)) + [0]
    smalls = (active, light_vector, class_gain[None], class_bias[None])
    table, ready, waiting, layers = None, near, [], []
    views = light_vector.shape[0]
    for index, shift in enumerate(shifts):
        first, last = index == 0, index + 1 == len(shifts)
        if first:
            table, *matter = matter_of(field, shift, smalls=smalls)
        else:
            matter = matter_of(field, shift, table=table, after=ready)
        if len(waiting) > 1:
            ready, = merge_of(*waiting.pop(0), matter[0], ready, slices, False)
            layers.append(passed_round(ready, "depth", shifts[len(layers)]))
        sources = field, matter, table, near, beyond
        if first or last:
            over, = prints_of(*sources, ready, shift, views, "over")
            ready = over
        else:
            own, over = prints_of(*sources, ready, shift, views, "all")
            ready = own
        if index == 1 or last and waiting:
            ready, *passed = merge_of(*waiting.pop(0), over if last else ready, ready, slices, last)
            over = passed[0] if last else over
            layers.append(passed_round(ready, "depth", shifts[len(layers)]))
        if first or last:
            own, = prints_of(*sources, ready, shift, views, "own")
            ready = own if first else ready
        waiting.append((own, passed_round(over, "tile", 1)))
    mix = early_of(depth_order, *waiting[0], [open_of(layers[0])] + layers[1:-1], shifts[:-1], slices)
    blocks = final_of(mix, layers[-1], share)
    blocks = lax.all_to_all(blocks, "tile", split_axis=0, concat_axis=0, tiled=True)
    return place_of(blocks)


def solution(mesh):
    placed = (P(None, "depth", "tile"), P("depth", "tile"), P(), P(), P(), P())
    return jax.shard_map(
        local,
        mesh=mesh,
        in_specs=placed,
        out_specs=P(None, None, ("depth", "tile"), None),
        check_vma=False,
    )
```
